32 devices in a mesh: gx: 2 (over y), gy: 4 (over x, core), gz: 4 (over z).
Axes of the slice: x: 2, y: 2, z: 4, core: 2. Of those that a mesh axis runs over, the one named last changes fastest.
Arguments:
- element_load: float32 [20, 68, 256], P('gz', 'gy', 'gx'), may hold values from -6 to 6
- conductivity: float32 [8, 32, 128], P('gz', 'gy', 'gx'), may hold values from 0.2 to 5
Outputs:
- corrected: float32 [20, 68, 256], P('gz', 'gy', 'gx')
The draws below stay inside these ranges and needn't reach their ends.
All inputs are finite; a program needn't handle non-finite values.
Results may differ from the reference program's by a relative error of at most 0.00002.
Values sent between devices are 32-bit elements; how exact they have to be, the bound alone decides.
A program may use at most 64 MiB of HBM per device.

```python
import math
import jax
import jax.numpy as jnp
import numpy as np
from jax import lax

DEG1 = 3
DEG2 = 4
NODES_Z = 20
NODES_Y = 68
NODES_X = 256
CELLS_Z = 8
CELLS_Y = 32
CELLS_X = 128
N_GX = 2
N_GY = 4
N_GZ = 4


def levels(rng, dims, split, low, top_value):
    gain, own = 1.0, jax.random.fold_in(rng, 6)
    for axis_at, blocks in split:
        steps = jnp.exp(jax.random.uniform(jax.random.fold_in(own, axis_at), (blocks,), jnp.float32, low / len(split), top_value / len(split)))
        gain = gain * jnp.repeat(steps, dims[axis_at] // blocks).reshape([-1 if axis == axis_at else 1 for axis in range(len(dims))])
    return gain


def noise(stream_key, shape, scale, reach, cuts=(), kind=jnp.bfloat16):
    loudness = levels(stream_key, shape, cuts, -0.22, 0.18) if cuts else 1.0
    values = jax.random.normal(stream_key, shape, jnp.float32) * scale * loudness
    return jnp.minimum(jnp.maximum(values, -reach), reach).astype(kind)


def setup_inputs(seed: int = 0) -> dict:
    key_of = jax.random.split(jax.random.key(seed), 3)
    return {
        "element_load": noise(key_of[0], (NODES_Z, NODES_Y, NODES_X), 1.0, 6.0, ((0, 4), (1, 4), (2, 2)), jnp.float32),
        "conductivity": jnp.clip(jnp.exp(math.log(5.0) - 3.218876 * jax.random.uniform(key_of[1], (CELLS_Z, CELLS_Y, CELLS_X), jnp.float32) ** levels(key_of[1], (CELLS_Z, CELLS_Y, CELLS_X), ((0, 4), (1, 4), (2, 2)), -0.2, 0.2)), 0.2, 5.0),
    }


reaction_rate = 0.05
lower_bound = 0.25
upper_bound = 2.5
mass_table = [[4.0 / 30.0, 2.0 / 30.0, -1.0 / 30.0], [2.0 / 30.0, 16.0 / 30.0, 2.0 / 30.0], [-1.0 / 30.0, 2.0 / 30.0, 4.0 / 30.0]]
stiff_table = [[7.0 / 3.0, -8.0 / 3.0, 1.0 / 3.0], [-8.0 / 3.0, 16.0 / 3.0, -8.0 / 3.0], [1.0 / 3.0, -8.0 / 3.0, 7.0 / 3.0]]


def pad_axis(values, which_axis, before, after):
    widths = [(0, 0)] * values.ndim
    widths[which_axis] = (before, after)
    return jnp.pad(values, widths)


def contract(values, matrix, which_axis):
    pieces = [lax.index_in_dim(values, a, which_axis, keepdims=False) for a in range(3)]
    results = [matrix[b][0] * pieces[0] + matrix[b][1] * pieces[1] + matrix[b][2] * pieces[2] for b in range(3)]
    return jnp.stack(results, axis=which_axis)


def node_slices(node_field, which_axis, periodic):
    if periodic:
        length_here = node_field.shape[which_axis]
        even_nodes = lax.slice_in_dim(node_field, 0, length_here, 2, axis=which_axis)
        odd_nodes = lax.slice_in_dim(node_field, 1, length_here, 2, axis=which_axis)
        return [even_nodes, odd_nodes, jnp.roll(even_nodes, -1, axis=which_axis)]
    elements = (node_field.shape[which_axis] - 1) // 2
    return [lax.slice_in_dim(node_field, a, a + 2 * elements - 1, 2, axis=which_axis) for a in range(3)]


def spread(node_field, periodic):
    along_x = jnp.stack(node_slices(node_field, 2, periodic), 0)
    along_y = jnp.stack(node_slices(along_x, 2, False), 1)
    return jnp.stack(node_slices(along_y, 2, False), 2)


def fold_back(stacked, which_axis, periodic):
    lower_part = stacked[0]
    middle_part = stacked[1]
    upper_part = stacked[2]
    target = which_axis - 1
    elements = lower_part.shape[target]
    if periodic:
        even_nodes = lower_part + jnp.roll(upper_part, 1, axis=target)
    else:
        even_full = pad_axis(lower_part, target, 0, 1) + pad_axis(upper_part, target, 1, 0)
        even_nodes = lax.slice_in_dim(even_full, 0, elements, axis=target)
        tail_node = lax.slice_in_dim(even_full, elements, elements + 1, axis=target)
    woven_nodes = jnp.stack([even_nodes, middle_part], axis=target + 1)
    node_shape = list(even_nodes.shape)
    node_shape[target] = 2 * elements
    woven_nodes = woven_nodes.reshape(node_shape)
    if periodic:
        return woven_nodes
    return jnp.concatenate([woven_nodes, tail_node], axis=target)


def gather_elements(product, periodic):
    folded = fold_back(product, 5, periodic)
    folded = fold_back(folded, 3, False)
    return fold_back(folded, 1, False)


def apply_local(node_field, conduct, stiff_scale, mass_scale, periodic):
    node_values = spread(node_field, periodic)
    mass_depth = contract(node_values, mass_table, 2)
    mass_plane = contract(mass_depth, mass_table, 1)
    stiffness = contract(mass_plane, stiff_table, 0)
    mass_width = contract(node_values, mass_table, 0)
    stiffness = stiffness + contract(contract(mass_width, stiff_table, 1), mass_table, 2)
    mass_face = contract(mass_width, mass_table, 1)
    stiffness = stiffness + contract(mass_face, stiff_table, 2)
    product = (stiff_scale * conduct) * stiffness + mass_scale * contract(mass_face, mass_table, 2)
    return gather_elements(product, periodic)


def diag_tables():
    stiff_line = np.array([stiff_table[a][a] for a in range(3)])
    mass_line = np.array([mass_table[a][a] for a in range(3)])
    stiff_part = (stiff_line[:, None, None] * mass_line[None, :, None] * mass_line[None, None, :]
                  + mass_line[:, None, None] * stiff_line[None, :, None] * mass_line[None, None, :]
                  + mass_line[:, None, None] * mass_line[None, :, None] * stiff_line[None, None, :])
    mass_part = mass_line[:, None, None] * mass_line[None, :, None] * mass_line[None, None, :]
    return stiff_part.reshape(3, 3, 3, 1, 1, 1), mass_part.reshape(3, 3, 3, 1, 1, 1)


def diag_local(conduct, stiff_scale, mass_scale, periodic):
    stiff_part, mass_part = diag_tables()
    product = (stiff_scale * conduct) * jnp.asarray(stiff_part, conduct.dtype) + mass_scale * jnp.asarray(mass_part, conduct.dtype)
    return gather_elements(product, periodic)


def coarse_conduct(conduct):
    layers_z, rows_y, cols_x = conduct.shape
    shaped = conduct.reshape(layers_z // 2, 2, rows_y // 2, 2, cols_x // 2, 2)
    return jnp.sum(shaped, axis=(1, 3, 5)) * 0.125


def prolong_axis(coarse, which_axis):
    pieces = node_slices(coarse, which_axis, False)
    fine_parts = [pieces[0],
                  0.375 * pieces[0] + 0.75 * pieces[1] - 0.125 * pieces[2],
                  pieces[1],
                  -0.125 * pieces[0] + 0.75 * pieces[1] + 0.375 * pieces[2]]
    woven_nodes = jnp.stack(fine_parts, axis=which_axis + 1)
    node_shape = list(pieces[0].shape)
    node_shape[which_axis] = 4 * pieces[0].shape[which_axis]
    woven_nodes = woven_nodes.reshape(node_shape)
    length_here = coarse.shape[which_axis]
    tail_node = lax.slice_in_dim(coarse, length_here - 1, length_here, axis=which_axis)
    return jnp.concatenate([woven_nodes, tail_node], axis=which_axis)


def prolong_all(coarse):
    result = prolong_axis(coarse, 0)
    result = prolong_axis(result, 1)
    return prolong_axis(result, 2)


def restrict_axis(fine, which_axis):
    length_here = fine.shape[which_axis]
    elements = (length_here - 1) // 4
    quarters = [lax.slice_in_dim(fine, q, q + 4 * elements - 3, 4, axis=which_axis) for q in range(4)]
    coarse_parts = [quarters[0] + 0.375 * quarters[1] - 0.125 * quarters[3],
                    0.75 * quarters[1] + quarters[2] + 0.75 * quarters[3],
                    -0.125 * quarters[1] + 0.375 * quarters[3]]
    folded = fold_back(jnp.stack(coarse_parts, 0), which_axis + 1, False)
    tail_node = lax.slice_in_dim(fine, length_here - 1, length_here, axis=which_axis)
    return folded + pad_axis(tail_node, which_axis, 2 * elements, 0)


def restrict_all(fine):
    result = restrict_axis(fine, 0)
    result = restrict_axis(result, 1)
    return restrict_axis(result, 2)


def chebyshev(right_side, diagonal, operate, degree):
    centre = 0.5 * (upper_bound + lower_bound)
    half_width = 0.5 * (upper_bound - lower_bound)
    sharpness = centre / half_width
    factor = 1.0 / sharpness
    scaled = 1.0 / diagonal
    update = (scaled * right_side) * (1.0 / centre)
    solution = update
    for k in range(1, degree):
        residual = right_side - operate(solution)
        next_factor = 1.0 / (2.0 * sharpness - factor)
        update = (next_factor * factor) * update + (2.0 * next_factor / half_width) * (scaled * residual)
        solution = solution + update
        factor = next_factor
    return solution


def to_blocks(global_array, splits):
    shaped = global_array.reshape(splits[0], global_array.shape[0] // splits[0], splits[1],
                                  global_array.shape[1] // splits[1], splits[2], global_array.shape[2] // splits[2])
    return shaped.transpose(0, 2, 4, 1, 3, 5)


def from_blocks(blocks):
    sizes_all = blocks.shape
    shaped = blocks.transpose(0, 3, 1, 4, 2, 5)
    return shaped.reshape(sizes_all[0] * sizes_all[3], sizes_all[1] * sizes_all[4], sizes_all[2] * sizes_all[5])


def per_device(function, arrays):
    def one_slab(slab_arrays):
        return jax.vmap(jax.vmap(function))(slab_arrays)

    return lax.map(one_slab, arrays)


def assemble_blocks(blocks):
    for p, q in ((0, 3), (1, 4), (2, 5)):
        length_here = blocks.shape[q]
        main_part = lax.slice_in_dim(blocks, 0, length_here - 1, axis=q)
        tail_part = lax.slice_in_dim(blocks, length_here - 1, length_here, axis=q)
        first_layer = lax.slice_in_dim(main_part, 0, 1, axis=q) + jnp.roll(tail_part, 1, axis=p)
        main_part = jnp.concatenate([first_layer, lax.slice_in_dim(main_part, 1, length_here - 1, axis=q)], axis=q)
        blocks = jnp.concatenate([main_part, jnp.roll(lax.slice_in_dim(main_part, 0, 1, axis=q), -1, axis=p)], axis=q)
    return blocks


def reference(element_load, conductivity):
    splits = (N_GZ, N_GY, N_GX)
    load_blocks = pad_axis(to_blocks(element_load, splits), 5, 0, 1)
    cond_blocks = to_blocks(conductivity, splits)
    diag_blocks = per_device(lambda members: diag_local(members[0], 1.0, reaction_rate, False), (cond_blocks,))
    right_side = assemble_blocks(load_blocks)
    diagonal = assemble_blocks(diag_blocks)

    def local_fine(node_field):
        return per_device(lambda members: apply_local(members[0], members[1], 1.0, reaction_rate, False), (node_field, cond_blocks))

    def operate_fine(node_field):
        return assemble_blocks(local_fine(node_field))

    smooth = chebyshev(right_side, diagonal, operate_fine, DEG1)
    partial_value = load_blocks - local_fine(smooth)
    coarse_load = per_device(lambda members: restrict_all(members[0]), (partial_value,))
    coarse_cond = per_device(lambda members: coarse_conduct(members[0]), (cond_blocks,))
    coarse_mass = 8.0 * reaction_rate
    coarse_diag = per_device(lambda members: diag_local(members[0], 2.0, coarse_mass, False), (coarse_cond,))

    def operate_coarse(node_field):
        return assemble_blocks(per_device(lambda members: apply_local(members[0], members[1], 2.0, coarse_mass, False), (node_field, coarse_cond)))

    correction = chebyshev(assemble_blocks(coarse_load), assemble_blocks(coarse_diag), operate_coarse, DEG2)
    corrected = smooth + per_device(lambda members: prolong_all(members[0]), (correction,))
    trimmed = corrected[:, :, :, :, :, : corrected.shape[5] - 1]
    return from_blocks(trimmed)
```

```python
import functools

import jax
import jax.numpy as jnp
from jax import lax
from jax.experimental import pallas as pl
from jax.experimental.pallas import tpu as pltpu
from jax.sharding import PartitionSpec as P

DEG1 = 3
DEG2 = 4
REACTION = 0.05
LOWER = 0.25
UPPER = 2.5
EIG = (0.0, 12.0, 60.0)
W = (1.0 / 36.0, 1.0 / 12.0, 1.0 / 45.0)
MESH = pl.DeviceIdType.MESH
STEPS = ((1, 0), (-1, 0), (0, 1), (0, -1), (1, 1), (1, -1), (-1, 1), (-1, -1))


def iota(shape, dim):
    return lax.broadcasted_iota(jnp.int32, shape, dim)


def dot(a, b):
    return jnp.dot(a, b, precision=lax.Precision.HIGHEST, preferred_element_type=jnp.float32)


def weight(d, odd):
    a = jnp.abs(d)
    even_w = jnp.where(a == 0, 1.0, jnp.where(a == 1, 0.375, jnp.where(a == 3, -0.125, 0.0)))
    odd_w = jnp.where(a == 0, 1.0, jnp.where(a == 1, 0.75, 0.0))
    return jnp.where(odd, odd_w, even_w)


def wrapped(d, period):
    d = jnp.where(d > period // 2, d - period, d)
    return jnp.where(d < -(period // 2), d + period, d)


def x_matrices(lanes):
    n = 2 * lanes
    r, c = iota((n, n), 0), iota((n, n), 1)
    split = jnp.where(r == 2 * (c % lanes) + c // lanes, 1.0, 0.0)
    q, e = r % 128, (r // 128) * 64 + r % 128
    hit = ((c < lanes) & (e == c)) | ((c >= lanes) & (e // 2 == c % (lanes // 2)))
    place = jnp.where((q < 64) & hit, 1.0, 0.0)
    node = 2 * (r % lanes) + r // lanes
    cp, m = c // lanes, c % (lanes // 2)
    restrict = weight(wrapped(node - 4 * m - 2 * cp, n), cp == 1)
    r, c = iota((n, 128), 0), iota((n, 128), 1)
    merge = jnp.where(2 * (r % lanes) + r // lanes == c, 1.0, 0.0)
    cp, m = r // lanes, r % lanes
    prolong = jnp.where(
        m < lanes // 2, weight(wrapped(c - 4 * m - 2 * cp, n), cp == 1), 0.0
    )
    return split, place, restrict, jnp.concatenate([merge, prolong], 1)


def fine_row(r):
    kind, i = r // 8, r % 8
    return jnp.where(kind == 2, jnp.where(i == 7, 16, 1000), 2 * i + kind)


def coarse_row(r):
    kind, i = r // 8, r % 8
    low = jnp.where(i < 4, 4 * i + 2 * kind, -1000)
    return jnp.where(kind == 2, jnp.where(i == 3, 16, -1000), low), kind == 1


def y_matrices():
    r, c = iota((24, 24), 0), iota((24, 24), 1)
    at, odd = coarse_row(r)
    restrict = weight(fine_row(c) - at, odd)
    at, odd = coarse_row(c)
    prolong = weight(r - at, odd)
    merge = jnp.where(fine_row(c) == r, 1.0, 0.0)
    return restrict, jnp.concatenate([merge, prolong], 1)


def roll_x(v, step):
    lanes = v.shape[-1]
    return pltpu.roll(v.reshape(-1, lanes), step % lanes, 1).reshape(v.shape)


def roll_y(v, step):
    flat = v.reshape((-1,) + v.shape[-2:])
    return pltpu.roll(flat, step % 8, 1).reshape(v.shape)


def forward(a, b, c):
    s = a + c
    return s + 4.0 * b, a - c, s - 2.0 * b


def backward(a, b, c, squared):
    s = a + c
    if squared:
        return s + b, 16.0 * a + 4.0 * c, s + b
    return s + b, 4.0 * a - 2.0 * c, s - b


def factors(cond, h):
    cells = cond.shape[0]
    out = []
    for l in range(3):
        rows = []
        for z in range(cells):
            for j in range(3):
                for i in range(3):
                    w = W[i] * W[j] * W[l]
                    rows.append(
                        cond[z] * (w * h * (EIG[i] + EIG[j] + EIG[l])) + w * REACTION * h**3
                    )
        out.append(jnp.stack(rows, 0).reshape((cells, 3, 3) + cond.shape[1:]))
    return out


def to_nodes(modes, squared=False):
    cells = modes[0].shape[0]
    row = iota(modes[0].shape[-2:], 0)
    low, mid, up = backward(*modes, squared)
    layers = [low[0]]
    for z in range(cells):
        layers.append(mid[z])
        layers.append(up[z] + low[z + 1] if z + 1 < cells else up[z])
    q = jnp.stack(layers, 0)
    low, mid, up = backward(q[:, 0], q[:, 1], q[:, 2], squared)
    even = low + jnp.where(row == 0, 0.0, roll_y(up, 1))
    q = jnp.stack([even, mid, up], 2)
    low, mid, up = backward(q[:, 0], q[:, 1], q[:, 2], squared)
    return low + roll_x(up, 1), mid


def apply_local(field, factor, ny):
    even, odd = field
    cells = factor[0].shape[0]
    row = iota(even.shape[-2:], 0)
    g = jnp.stack(forward(even, odd, roll_x(even, -1)), 0)
    low, mid, end = g[:, :, 0], g[:, :, 1], g[:, :, 2]
    up = jnp.where(row == ny - 1, end, roll_y(low, -1))
    y = jnp.stack(forward(low, mid, up), 0)
    parts = [jnp.stack([y[:, :, 2 * z + a] for z in range(cells)], 0) for a in range(3)]
    modes = forward(*parts)
    return to_nodes([m * f for m, f in zip(modes, factor)])


def exchange(fields, phase, ny, bufs):
    zs, zr, ys, yr, cs, cr, send_sem, recv_sem = bufs
    flat = [part for field in fields for part in field]
    count = len(flat)
    layers = flat[0].shape[0]
    last = layers - 1
    row = iota(flat[0].shape[-2:], 0)
    for f, part in enumerate(flat):
        zs[phase, 0, f] = part[last]
        zs[phase, 1, f] = part[0]
        for l in range(layers):
            ys[phase, 0, f, l : l + 1] = part[l, 2, ny - 1 : ny]
            ys[phase, 1, f, l : l + 1] = part[l, 0, 0:1]
        cs[phase, 0, f : f + 1] = part[last, 2, ny - 1 : ny]
        cs[phase, 1, f : f + 1] = part[0, 2, ny - 1 : ny]
        cs[phase, 2, f : f + 1] = part[last, 0, 0:1]
        cs[phase, 3, f : f + 1] = part[0, 0, 0:1]
    gy, gz = lax.axis_size("gy"), lax.axis_size("gz")
    iy, iz = lax.axis_index("gy"), lax.axis_index("gz")
    copies = []
    for k in (2, 3, 0, 1, 4, 5, 6, 7):
        dy, dz = STEPS[k]
        if k < 2:
            src, dst = ys.at[phase, k, pl.ds(0, count)], yr.at[phase, k, pl.ds(0, count)]
        elif k < 4:
            src, dst = zs.at[phase, k - 2, pl.ds(0, count)], zr.at[phase, k - 2, pl.ds(0, count)]
        else:
            src, dst = cs.at[phase, k - 4], cr.at[phase, k - 4]
        copy = pltpu.make_async_remote_copy(
            src_ref=src,
            dst_ref=dst,
            send_sem=send_sem.at[phase, k],
            recv_sem=recv_sem.at[phase, k],
            device_id={"gy": lax.rem(iy + dy + gy, gy), "gz": lax.rem(iz + dz + gz, gz)},
            device_id_type=MESH,
        )
        copy.start()
        copies.append(copy)
    for copy in copies:
        copy.wait_recv()
    out = []
    for f, part in enumerate(flat):
        done = []
        for l in range(layers):
            first = yr[phase, 0, f, l : l + 1]
            end = yr[phase, 1, f, l : l + 1]
            if l == last:
                first = first + cr[phase, 1, f : f + 1]
                end = end + cr[phase, 3, f : f + 1]
            if l == 0:
                first = first + cr[phase, 0, f : f + 1]
                end = end + cr[phase, 2, f : f + 1]
            low = part[l, 0] + jnp.where(row == 0, first, 0.0)
            layer = jnp.stack([low, part[l, 1], part[l, 2] + end], 0)
            if l == 0:
                layer = layer + zr[phase, 0, f]
            if l == last:
                layer = layer + zr[phase, 1, f]
            done.append(layer)
        out.append(jnp.stack(done, 0))
    return [(out[2 * i], out[2 * i + 1]) for i in range(len(fields))], copies


def inverse(diagonal, ny):
    row = iota(diagonal.shape[-2:], 0)
    whole = jnp.where(row < ny, 1.0 / diagonal[:, 0:2], 0.0)
    end = jnp.where(row == ny - 1, 1.0 / diagonal[:, 2:3], 0.0)
    return jnp.concatenate([whole, end], 1)


def chebyshev(right, diagonal, factor, degree, ny, phase, bufs):
    centre = 0.5 * (UPPER + LOWER)
    half = 0.5 * (UPPER - LOWER)
    sharp = centre / half
    f = 1.0 / sharp
    scaled = [inverse(d, ny) for d in diagonal]
    update = [s * r * (1.0 / centre) for s, r in zip(scaled, right)]
    total = update
    started = []
    for k in range(1, degree):
        (image,), copies = exchange([apply_local(total, factor, ny)], phase + k - 1, ny, bufs)
        started += copies
        g = 1.0 / (2.0 * sharp - f)
        update = [
            (g * f) * u + (2.0 * g / half) * (s * (r - a))
            for u, s, r, a in zip(update, scaled, right, image)
        ]
        total = [t + u for t, u in zip(total, update)]
        f = g
    return total, started


def kernel(load_ref, cond_ref, out_ref, line, cells, cell_out, zs, zr, ys, yr, cs, cr,
           send_sem, recv_sem, x_send, x_recv):
    gx, gy, gz = lax.axis_size("gx"), lax.axis_size("gy"), lax.axis_size("gz")
    ix, iy, iz = lax.axis_index("gx"), lax.axis_index("gy"), lax.axis_index("gz")
    lanes = 64 * gx
    bufs = (zs, zr, ys, yr, cs, cr, send_sem, recv_sem)
    barrier = pltpu.get_barrier_semaphore()
    for dy, dz in STEPS:
        pl.semaphore_signal(
            barrier, inc=1,
            device_id={"gy": lax.rem(iy + dy + gy, gy), "gz": lax.rem(iz + dz + gz, gz)},
            device_id_type=MESH,
        )
    for d in range(1, gx):
        pl.semaphore_signal(
            barrier, inc=1, device_id={"gx": lax.rem(ix + d, gx)}, device_id_type=MESH
        )
    cell_out[...] = jnp.zeros(cell_out.shape, jnp.float32)
    cell_out[:, :, 0:64] = cond_ref[...]
    pl.semaphore_wait(barrier, len(STEPS) + gx - 1)
    started = []
    arrivals = []
    for d in range(1, gx):
        for k, (src, dst) in enumerate(((load_ref, line), (cell_out, cells))):
            copy = pltpu.make_async_remote_copy(
                src_ref=src,
                dst_ref=dst.at[gx - d - 1],
                send_sem=x_send.at[k, d - 1],
                recv_sem=x_recv.at[k, gx - d - 1],
                device_id={"gx": lax.rem(ix + d, gx)},
                device_id_type=MESH,
            )
            copy.start()
            arrivals.append(copy)
    split, place, restrict_x, out_x = x_matrices(lanes)
    restrict_y, out_y = y_matrices()
    for copy in arrivals:
        copy.wait_recv()
    started += arrivals

    def rows(ref):
        parts = []
        for z in range(5):
            parts.append(ref[z, pl.ds(0, 8, stride=2), :])
            parts.append(ref[z, pl.ds(1, 8, stride=2), :])
            parts.append(jnp.broadcast_to(ref[z, 16:17, :], (8, 128)))
        return jnp.concatenate(parts, 0)

    joined = jnp.concatenate(
        [rows(load_ref)] + [rows(line.at[d]) for d in range(gx - 1)], 1
    )
    loads = dot(joined, split)
    load = (loads[:, :lanes].reshape(5, 3, 8, lanes), loads[:, lanes:].reshape(5, 3, 8, lanes))
    joined = jnp.concatenate(
        [cell_out[...].reshape(16, 128)] + [cells[d].reshape(16, 128) for d in range(gx - 1)], 1
    )
    conds = dot(joined, place)
    cond = conds[:, :lanes].reshape(2, 8, lanes)
    pair = conds[:8, lanes:] + conds[8:, lanes:]
    r, c = iota((8, 8), 0), iota((8, 8), 1)
    coarse_cond = dot(jnp.where(c // 2 == r, 0.125, 0.0), pair).reshape(1, 8, lanes)

    fine = factors(cond, 1.0)
    (right, diagonal), copies = exchange([load, to_nodes(fine, True)], 0, 8, bufs)
    started += copies
    smooth, copies = chebyshev(right, diagonal, fine, DEG1, 8, 1, bufs)
    started += copies
    image = apply_local(smooth, fine, 8)
    part = [
        jnp.concatenate([(b - a).reshape(5, 24, lanes) for b, a in zip(load, image)], 2)
    ][0]
    f0, f1, f2, f3, f4 = (part[z] for z in range(5))
    three = jnp.concatenate(
        [
            f0 + 0.375 * f1 - 0.125 * f3,
            0.75 * f1 + f2 + 0.75 * f3,
            -0.125 * f1 + 0.375 * f3 + f4,
        ],
        0,
    )
    three = dot(three, restrict_x).reshape(3, 24, 2 * lanes)
    wide = dot(restrict_y, jnp.concatenate([three[z] for z in range(3)], 1))
    coarse_load = tuple(
        jnp.stack(
            [
                wide[:, (2 * z + p) * lanes : (2 * z + p + 1) * lanes].reshape(3, 8, lanes)
                for z in range(3)
            ],
            0,
        )
        for p in range(2)
    )
    coarse = factors(coarse_cond, 2.0)
    (right, diagonal), copies = exchange(
        [coarse_load, to_nodes(coarse, True)], DEG1, 4, bufs
    )
    started += copies
    correction, copies = chebyshev(right, diagonal, coarse, DEG2, 4, DEG1 + 1, bufs)
    started += copies

    own = jnp.concatenate([s.reshape(120, lanes) for s in smooth], 1)
    own = dot(own, out_x[:, :128])
    both = jnp.concatenate([s.reshape(3, 24, lanes) for s in correction], 2)
    c0, c1, c2 = both[0], both[1], both[2]
    five = jnp.concatenate(
        [
            c0,
            0.375 * c0 + 0.75 * c1 - 0.125 * c2,
            c1,
            -0.125 * c0 + 0.75 * c1 + 0.375 * c2,
            c2,
        ],
        0,
    )
    five = dot(five, out_x[:, 128:])
    tall = jnp.concatenate(
        [
            jnp.concatenate([v[24 * z : 24 * z + 24] for z in range(5)], 1)
            for v in (own, five)
        ],
        0,
    )
    result = dot(out_y, tall)
    for z in range(5):
        out_ref[z] = result[0:17, 128 * z : 128 * z + 128]
    for copy in started:
        copy.wait_send()


def solution(mesh):
    gx = mesh.shape["gx"]
    lanes = 64 * gx
    phases = DEG1 + DEG2

    def step(element_load, conductivity):
        vmem = pl.BlockSpec(memory_space=pltpu.VMEM)
        f32 = jnp.float32
        return pl.pallas_call(
            kernel,
            out_shape=jax.ShapeDtypeStruct(element_load.shape, f32),
            in_specs=[vmem, vmem],
            out_specs=vmem,
            scratch_shapes=[
                pltpu.VMEM((gx - 1,) + element_load.shape, f32),
                pltpu.VMEM((gx - 1, 2, 8, 128), f32),
                pltpu.VMEM((2, 8, 128), f32),
                pltpu.VMEM((phases, 2, 4, 3, 8, lanes), f32),
                pltpu.VMEM((phases, 2, 4, 3, 8, lanes), f32),
                pltpu.VMEM((phases, 2, 4, 8, lanes), f32),
                pltpu.VMEM((phases, 2, 4, 8, lanes), f32),
                pltpu.VMEM((phases, 4, 8, lanes), f32),
                pltpu.VMEM((phases, 4, 8, lanes), f32),
                pltpu.SemaphoreType.DMA((phases, 8)),
                pltpu.SemaphoreType.DMA((phases, 8)),
                pltpu.SemaphoreType.DMA((2, gx - 1)),
                pltpu.SemaphoreType.DMA((2, gx - 1)),
            ],
            compiler_params=pltpu.CompilerParams(
                collective_id=0, has_side_effects=True, vmem_limit_bytes=48 * 1024 * 1024
            ),
        )(element_load, conductivity)

    spec = P("gz", "gy", "gx")
    return jax.shard_map(
        step, mesh=mesh, in_specs=(spec, spec), out_specs=spec, check_vma=False
    )
```

```python
import functools

import jax
import jax.numpy as jnp
from jax import lax
from jax.experimental import pallas as pl
from jax.experimental.pallas import tpu as pltpu
from jax.sharding import PartitionSpec as P

DEG1 = 3
DEG2 = 4
REACTION = 0.05
LOWER = 0.25
UPPER = 2.5
EIG = (0.0, 12.0, 60.0)
W = (1.0 / 36.0, 1.0 / 12.0, 1.0 / 45.0)
MESH = pl.DeviceIdType.MESH
STEPS = ((1, 0), (-1, 0), (0, 1), (0, -1), (1, 1), (1, -1), (-1, 1), (-1, -1))


def iota(shape, dim):
    return lax.broadcasted_iota(jnp.int32, shape, dim)


def pieces(v):
    high = v.astype(jnp.bfloat16).astype(jnp.float32)
    rest = v - high
    mid = rest.astype(jnp.bfloat16).astype(jnp.float32)
    return [high, mid, rest - mid]


def dot_right(v, matrix):
    n = v.shape[0]
    tall = jnp.concatenate(pieces(v), 0).astype(jnp.bfloat16)
    out = jnp.dot(tall, matrix, preferred_element_type=jnp.float32)
    return out[2 * n :] + out[n : 2 * n] + out[:n]


def dot_left(matrix, v):
    tall = jnp.concatenate(pieces(v), 0).astype(jnp.bfloat16)
    wide = jnp.concatenate([matrix] * 3, 1).astype(jnp.bfloat16)
    return jnp.dot(wide, tall, preferred_element_type=jnp.float32)


def weight(d, odd):
    a = jnp.abs(d)
    even_w = jnp.where(a == 0, 1.0, jnp.where(a == 1, 0.375, jnp.where(a == 3, -0.125, 0.0)))
    odd_w = jnp.where(a == 0, 1.0, jnp.where(a == 1, 0.75, 0.0))
    return jnp.where(odd, odd_w, even_w)


def wrapped(d, period):
    d = jnp.where(d > period // 2, d - period, d)
    return jnp.where(d < -(period // 2), d + period, d)


def bits(n):
    return n.bit_length() - 1


def split_matrix(lanes):
    n = 2 * lanes
    r, c = iota((n, n), 0), iota((n, n), 1)
    return jnp.where(r == 2 * (c & (lanes - 1)) + (c >> bits(lanes)), 1.0, 0.0).astype(jnp.bfloat16)


def place_matrix(lanes):
    n = 2 * lanes
    r, c = iota((n, n), 0), iota((n, n), 1)
    q, e = r & 127, ((r >> 7) << 6) + (r & 127)
    hit = ((c < lanes) & (e == c)) | ((c >= lanes) & ((e >> 1) == (c & (lanes // 2 - 1))))
    return jnp.where((q < 64) & hit, 1.0, 0.0).astype(jnp.bfloat16)


def restrict_matrix(lanes):
    n = 2 * lanes
    r, c = iota((n, n), 0), iota((n, n), 1)
    node = 2 * (r & (lanes - 1)) + (r >> bits(lanes))
    cp, m = c >> bits(lanes), c & (lanes // 2 - 1)
    return weight(wrapped(node - 4 * m - 2 * cp, n), cp == 1).astype(jnp.bfloat16)


def out_matrix(lanes):
    n = 2 * lanes
    r, c = iota((n, 128), 0), iota((n, 128), 1)
    m, cp = r & (lanes - 1), r >> bits(lanes)
    merge = jnp.where(2 * m + cp == c, 1.0, 0.0)
    prolong = jnp.where(
        m < lanes // 2, weight(wrapped(c - 4 * m - 2 * cp, n), cp == 1), 0.0
    )
    return jnp.concatenate([merge, prolong], 1).astype(jnp.bfloat16)


def fine_row(r):
    kind, i = r >> 3, r & 7
    return jnp.where(kind == 2, jnp.where(i == 7, 16, 1000), 2 * i + kind)


def coarse_row(r):
    kind, i = r >> 3, r & 7
    low = jnp.where(i < 4, 4 * i + 2 * kind, -1000)
    return jnp.where(kind == 2, jnp.where(i == 3, 16, -1000), low), kind == 1


def y_matrices():
    r, c = iota((24, 24), 0), iota((24, 24), 1)
    at, odd = coarse_row(r)
    restrict = weight(fine_row(c) - at, odd)
    at, odd = coarse_row(c)
    prolong = weight(r - at, odd)
    merge = jnp.where(fine_row(c) == r, 1.0, 0.0)
    return restrict, jnp.concatenate([merge, prolong], 1)


def roll_x(v, step):
    lanes = v.shape[-1]
    return pltpu.roll(v.reshape(-1, lanes), step % lanes, 1).reshape(v.shape)


def roll_y(v, step):
    flat = v.reshape((-1,) + v.shape[-2:])
    return pltpu.roll(flat, step % 8, 1).reshape(v.shape)


def forward(a, b, c):
    s = a + c
    return s + 4.0 * b, a - c, s - 2.0 * b


def backward(a, b, c, squared):
    s = a + c
    if squared:
        return s + b, 16.0 * a + 4.0 * c, s + b
    return s + b, 4.0 * a - 2.0 * c, s - b


def factors(cond, h):
    cells = cond.shape[0]
    out = []
    for l in range(3):
        rows = []
        for z in range(cells):
            for j in range(3):
                for i in range(3):
                    w = W[i] * W[j] * W[l]
                    rows.append(
                        cond[z] * (w * h * (EIG[i] + EIG[j] + EIG[l])) + w * REACTION * h**3
                    )
        out.append(jnp.stack(rows, 0).reshape((cells, 3, 3) + cond.shape[1:]))
    return out


def to_nodes(modes, squared=False):
    cells = modes[0].shape[0]
    row = iota(modes[0].shape[-2:], 0)
    low, mid, up = backward(*modes, squared)
    layers = [low[0]]
    for z in range(cells):
        layers.append(mid[z])
        layers.append(up[z] + low[z + 1] if z + 1 < cells else up[z])
    q = jnp.stack(layers, 0)
    low, mid, up = backward(q[:, 0], q[:, 1], q[:, 2], squared)
    even = low + jnp.where(row == 0, 0.0, roll_y(up, 1))
    q = jnp.stack([even, mid, up], 2)
    low, mid, up = backward(q[:, 0], q[:, 1], q[:, 2], squared)
    return low + roll_x(up, 1), mid


def apply_local(field, factor, ny):
    even, odd = field
    cells = factor[0].shape[0]
    row = iota(even.shape[-2:], 0)
    g = jnp.stack(forward(even, odd, roll_x(even, -1)), 0)
    low, mid, end = g[:, :, 0], g[:, :, 1], g[:, :, 2]
    up = jnp.where(row == ny - 1, end, roll_y(low, -1))
    y = jnp.stack(forward(low, mid, up), 0)
    parts = [jnp.stack([y[:, :, 2 * z + a] for z in range(cells)], 0) for a in range(3)]
    modes = forward(*parts)
    return to_nodes([m * f for m, f in zip(modes, factor)])


def exchange(fields, phase, ny, bufs, beside=None):
    zs, zr, ys, yr, cs, cr, send_sem, recv_sem = bufs
    flat = [part for field in fields for part in field]
    count = len(flat)
    layers = flat[0].shape[0]
    last = layers - 1
    row = iota(flat[0].shape[-2:], 0)
    for f, part in enumerate(flat):
        zs[phase, 0, f] = part[last]
        zs[phase, 1, f] = part[0]
        for l in range(layers):
            ys[phase, 0, f, l : l + 1] = part[l, 2, ny - 1 : ny]
            ys[phase, 1, f, l : l + 1] = part[l, 0, 0:1]
        cs[phase, 0, f : f + 1] = part[last, 2, ny - 1 : ny]
        cs[phase, 1, f : f + 1] = part[0, 2, ny - 1 : ny]
        cs[phase, 2, f : f + 1] = part[last, 0, 0:1]
        cs[phase, 3, f : f + 1] = part[0, 0, 0:1]
    gy, gz = lax.axis_size("gy"), lax.axis_size("gz")
    iy, iz = lax.axis_index("gy"), lax.axis_index("gz")
    copies = []
    for k in (2, 3, 0, 1, 4, 5, 6, 7):
        dy, dz = STEPS[k]
        if k < 2:
            src, dst = ys.at[phase, k, pl.ds(0, count)], yr.at[phase, k, pl.ds(0, count)]
        elif k < 4:
            src, dst = zs.at[phase, k - 2, pl.ds(0, count)], zr.at[phase, k - 2, pl.ds(0, count)]
        else:
            src, dst = cs.at[phase, k - 4], cr.at[phase, k - 4]
        copy = pltpu.make_async_remote_copy(
            src_ref=src,
            dst_ref=dst,
            send_sem=send_sem.at[phase, k],
            recv_sem=recv_sem.at[phase, k],
            device_id={"gy": lax.rem(iy + dy + gy, gy), "gz": lax.rem(iz + dz + gz, gz)},
            device_id_type=MESH,
        )
        copy.start()
        copies.append(copy)
    if beside is not None:
        beside()
    for copy in copies:
        copy.wait_recv()
    out = []
    for f, part in enumerate(flat):
        done = []
        for l in range(layers):
            first = yr[phase, 0, f, l : l + 1]
            end = yr[phase, 1, f, l : l + 1]
            if l == last:
                first = first + cr[phase, 1, f : f + 1]
                end = end + cr[phase, 3, f : f + 1]
            if l == 0:
                first = first + cr[phase, 0, f : f + 1]
                end = end + cr[phase, 2, f : f + 1]
            low = part[l, 0] + jnp.where(row == 0, first, 0.0)
            layer = jnp.stack([low, part[l, 1], part[l, 2] + end], 0)
            if l == 0:
                layer = layer + zr[phase, 0, f]
            if l == last:
                layer = layer + zr[phase, 1, f]
            done.append(layer)
        out.append(jnp.stack(done, 0))
    return [(out[2 * i], out[2 * i + 1]) for i in range(len(fields))], copies


def inverse(diagonal, ny):
    row = iota(diagonal.shape[-2:], 0)
    whole = jnp.where(row < ny, 1.0 / diagonal[:, 0:2], 0.0)
    end = jnp.where(row == ny - 1, 1.0 / diagonal[:, 2:3], 0.0)
    return jnp.concatenate([whole, end], 1)


def chebyshev(right, diagonal, factor, degree, ny, phase, bufs):
    centre = 0.5 * (UPPER + LOWER)
    half = 0.5 * (UPPER - LOWER)
    sharp = centre / half
    f = 1.0 / sharp
    scaled = [inverse(d, ny) for d in diagonal]
    update = [s * r * (1.0 / centre) for s, r in zip(scaled, right)]
    total = update
    started = []
    for k in range(1, degree):
        (image,), copies = exchange([apply_local(total, factor, ny)], phase + k - 1, ny, bufs)
        started += copies
        g = 1.0 / (2.0 * sharp - f)
        update = [
            (g * f) * u + (2.0 * g / half) * (s * (r - a))
            for u, s, r, a in zip(update, scaled, right, image)
        ]
        total = [t + u for t, u in zip(total, update)]
        f = g
    return total, started


def kernel(load_ref, cond_ref, out_ref, line, cells, cell_out, zs, zr, ys, yr, cs, cr,
           send_sem, recv_sem, x_send, x_recv, matrix_x, matrix_out):
    gx, gy, gz = lax.axis_size("gx"), lax.axis_size("gy"), lax.axis_size("gz")
    ix, iy, iz = lax.axis_index("gx"), lax.axis_index("gy"), lax.axis_index("gz")
    lanes = 64 * gx
    bufs = (zs, zr, ys, yr, cs, cr, send_sem, recv_sem)
    barrier = pltpu.get_barrier_semaphore()
    for dy, dz in STEPS:
        pl.semaphore_signal(
            barrier, inc=1,
            device_id={"gy": lax.rem(iy + dy + gy, gy), "gz": lax.rem(iz + dz + gz, gz)},
            device_id_type=MESH,
        )
    for d in range(1, gx):
        pl.semaphore_signal(
            barrier, inc=1, device_id={"gx": lax.rem(ix + d, gx)}, device_id_type=MESH
        )
    cell_out[...] = jnp.zeros(cell_out.shape, jnp.float32)
    cell_out[:, :, 0:64] = cond_ref[...]
    pl.semaphore_wait(barrier, len(STEPS) + gx - 1)
    started = []
    arrivals = []
    for d in range(1, gx):
        for k, (src, dst) in enumerate(((load_ref, line), (cell_out, cells))):
            copy = pltpu.make_async_remote_copy(
                src_ref=src,
                dst_ref=dst.at[gx - d - 1],
                send_sem=x_send.at[k, d - 1],
                recv_sem=x_recv.at[k, gx - d - 1],
                device_id={"gx": lax.rem(ix + d, gx)},
                device_id_type=MESH,
            )
            copy.start()
            arrivals.append(copy)
    split_x, place = split_matrix(lanes), place_matrix(lanes)
    for copy in arrivals:
        copy.wait_recv()
    started += arrivals

    def rows(ref):
        parts = []
        for z in range(5):
            parts.append(ref[z, pl.ds(0, 8, stride=2), :])
            parts.append(ref[z, pl.ds(1, 8, stride=2), :])
            parts.append(jnp.broadcast_to(ref[z, 16:17, :], (8, 128)))
        return jnp.concatenate(parts, 0)

    joined = jnp.concatenate(
        [rows(load_ref)] + [rows(line.at[d]) for d in range(gx - 1)], 1
    )
    loads = dot_right(joined, split_x)
    load = (loads[:, :lanes].reshape(5, 3, 8, lanes), loads[:, lanes:].reshape(5, 3, 8, lanes))
    joined = jnp.concatenate(
        [cell_out[...].reshape(16, 128)] + [cells[d].reshape(16, 128) for d in range(gx - 1)], 1
    )
    conds = dot_right(joined, place)
    cond = conds[:, :lanes].reshape(2, 8, lanes)
    pair = conds[:8, lanes:] + conds[8:, lanes:]
    r, c = iota((8, 8), 0), iota((8, 8), 1)
    coarse_cond = dot_left(jnp.where((c >> 1) == r, 0.125, 0.0), pair).reshape(1, 8, lanes)

    fine = factors(cond, 1.0)

    def fill():
        matrix_x[...] = restrict_matrix(lanes)
        matrix_out[...] = out_matrix(lanes)

    (right, diagonal), copies = exchange([load, to_nodes(fine, True)], 0, 8, bufs, fill)
    restrict_y, out_y = y_matrices()
    started += copies
    smooth, copies = chebyshev(right, diagonal, fine, DEG1, 8, 1, bufs)
    started += copies
    image = apply_local(smooth, fine, 8)
    part = [
        jnp.concatenate([(b - a).reshape(5, 24, lanes) for b, a in zip(load, image)], 2)
    ][0]
    f0, f1, f2, f3, f4 = (part[z] for z in range(5))
    three = jnp.concatenate(
        [
            f0 + 0.375 * f1 - 0.125 * f3,
            0.75 * f1 + f2 + 0.75 * f3,
            -0.125 * f1 + 0.375 * f3 + f4,
        ],
        0,
    )
    three = dot_right(three, matrix_x[...]).reshape(3, 24, 2 * lanes)
    wide = dot_left(restrict_y, jnp.concatenate([three[z] for z in range(3)], 1))
    coarse_load = tuple(
        jnp.stack(
            [
                wide[:, (2 * z + p) * lanes : (2 * z + p + 1) * lanes].reshape(3, 8, lanes)
                for z in range(3)
            ],
            0,
        )
        for p in range(2)
    )
    coarse = factors(coarse_cond, 2.0)
    (right, diagonal), copies = exchange(
        [coarse_load, to_nodes(coarse, True)], DEG1, 4, bufs
    )
    started += copies
    correction, copies = chebyshev(right, diagonal, coarse, DEG2, 4, DEG1 + 1, bufs)
    started += copies

    own = jnp.concatenate([s.reshape(120, lanes) for s in smooth], 1)
    own = dot_right(own, matrix_out[:, :128])
    both = jnp.concatenate([s.reshape(3, 24, lanes) for s in correction], 2)
    c0, c1, c2 = both[0], both[1], both[2]
    five = jnp.concatenate(
        [
            c0,
            0.375 * c0 + 0.75 * c1 - 0.125 * c2,
            c1,
            -0.125 * c0 + 0.75 * c1 + 0.375 * c2,
            c2,
        ],
        0,
    )
    five = dot_right(five, matrix_out[:, 128:])
    tall = jnp.concatenate(
        [
            jnp.concatenate([v[24 * z : 24 * z + 24] for z in range(5)], 1)
            for v in (own, five)
        ],
        0,
    )
    result = dot_left(out_y, tall)
    for z in range(5):
        out_ref[z] = result[0:17, 128 * z : 128 * z + 128]
    for copy in started:
        copy.wait_send()


def solution(mesh):
    gx = mesh.shape["gx"]
    lanes = 64 * gx
    phases = DEG1 + DEG2

    def step(element_load, conductivity):
        vmem = pl.BlockSpec(memory_space=pltpu.VMEM)
        f32 = jnp.float32
        return pl.pallas_call(
            kernel,
            out_shape=jax.ShapeDtypeStruct(element_load.shape, f32),
            in_specs=[vmem, vmem],
            out_specs=vmem,
            scratch_shapes=[
                pltpu.VMEM((gx - 1,) + element_load.shape, f32),
                pltpu.VMEM((gx - 1, 2, 8, 128), f32),
                pltpu.VMEM((2, 8, 128), f32),
                pltpu.VMEM((phases, 2, 4, 3, 8, lanes), f32),
                pltpu.VMEM((phases, 2, 4, 3, 8, lanes), f32),
                pltpu.VMEM((phases, 2, 4, 8, lanes), f32),
                pltpu.VMEM((phases, 2, 4, 8, lanes), f32),
                pltpu.VMEM((phases, 4, 8, lanes), f32),
                pltpu.VMEM((phases, 4, 8, lanes), f32),
                pltpu.SemaphoreType.DMA((phases, 8)),
                pltpu.SemaphoreType.DMA((phases, 8)),
                pltpu.SemaphoreType.DMA((2, gx - 1)),
                pltpu.SemaphoreType.DMA((2, gx - 1)),
                pltpu.VMEM((2 * lanes, 2 * lanes), jnp.bfloat16),
                pltpu.VMEM((2 * lanes, 256), jnp.bfloat16),
            ],
            compiler_params=pltpu.CompilerParams(
                collective_id=0, has_side_effects=True, vmem_limit_bytes=48 * 1024 * 1024
            ),
        )(element_load, conductivity)

    spec = P("gz", "gy", "gx")
    return jax.shard_map(
        step, mesh=mesh, in_specs=(spec, spec), out_specs=spec, check_vma=False
    )
```

```python
import functools

import jax
import jax.numpy as jnp
from jax import lax
from jax.experimental import pallas as pl
from jax.experimental.pallas import tpu as pltpu
from jax.sharding import PartitionSpec as P

DEG1 = 3
DEG2 = 4
REACTION = 0.05
LOWER = 0.25
UPPER = 2.5
EIG = (0.0, 12.0, 60.0)
W = (1.0 / 36.0, 1.0 / 12.0, 1.0 / 45.0)
MESH = pl.DeviceIdType.MESH
STEPS = ((1, 0), (-1, 0), (0, 1), (0, -1), (1, 1), (1, -1), (-1, 1), (-1, -1))


def iota(shape, dim):
    return lax.broadcasted_iota(jnp.int32, shape, dim)


def pieces(v):
    high = v.astype(jnp.bfloat16).astype(jnp.float32)
    rest = v - high
    mid = rest.astype(jnp.bfloat16).astype(jnp.float32)
    return [high, mid, rest - mid]


def dot_right(v, matrix):
    n = v.shape[0]
    tall = jnp.concatenate(pieces(v), 0).astype(jnp.bfloat16)
    out = jnp.dot(tall, matrix, preferred_element_type=jnp.float32)
    return out[2 * n :] + out[n : 2 * n] + out[:n]


def dot_left(matrix, v):
    tall = jnp.concatenate(pieces(v), 0).astype(jnp.bfloat16)
    wide = jnp.concatenate([matrix] * 3, 1).astype(jnp.bfloat16)
    return jnp.dot(wide, tall, preferred_element_type=jnp.float32)


def weight(d, odd):
    a = jnp.abs(d)
    even_w = jnp.where(a == 0, 1.0, jnp.where(a == 1, 0.375, jnp.where(a == 3, -0.125, 0.0)))
    odd_w = jnp.where(a == 0, 1.0, jnp.where(a == 1, 0.75, 0.0))
    return jnp.where(odd, odd_w, even_w)


def wrapped(d, period):
    d = jnp.where(d > period // 2, d - period, d)
    return jnp.where(d < -(period // 2), d + period, d)


def bits(n):
    return n.bit_length() - 1


def split_matrix(lanes):
    n = 2 * lanes
    r, c = iota((n, n), 0), iota((n, n), 1)
    return jnp.where(r == 2 * (c & (lanes - 1)) + (c >> bits(lanes)), 1.0, 0.0).astype(jnp.bfloat16)


def place_matrix(lanes):
    n = 2 * lanes
    r, c = iota((n, n), 0), iota((n, n), 1)
    q, e = r & 127, ((r >> 7) << 6) + (r & 127)
    hit = ((c < lanes) & (e == c)) | ((c >= lanes) & ((e >> 1) == (c & (lanes // 2 - 1))))
    return jnp.where((q < 64) & hit, 1.0, 0.0).astype(jnp.bfloat16)


def restrict_matrix(lanes):
    n = 2 * lanes
    r, c = iota((n, lanes), 0), iota((n, lanes), 1)
    node = 2 * (r & (lanes - 1)) + (r >> bits(lanes))
    cp, m = c >> bits(lanes // 2), c & (lanes // 2 - 1)
    return weight(wrapped(node - 4 * m - 2 * cp, n), cp == 1).astype(jnp.bfloat16)


def out_matrix(lanes):
    n = 2 * lanes
    r, c = iota((n, 128), 0), iota((n, 128), 1)
    m, cp = r & (lanes - 1), r >> bits(lanes)
    merge = jnp.where(2 * m + cp == c, 1.0, 0.0)
    prolong = jnp.where(
        m < lanes // 2, weight(wrapped(c - 4 * m - 2 * cp, n), cp == 1), 0.0
    )
    return jnp.concatenate([merge, prolong], 1).astype(jnp.bfloat16)


def fine_row(r):
    kind, i = r >> 3, r & 7
    return jnp.where(kind == 2, jnp.where(i == 7, 16, 1000), 2 * i + kind)


def packet_matrix():
    r, c = iota((32, 24), 0), iota((32, 24), 1)
    kind, i = (r & 7) >> 2, r & 3
    end = r >= 24
    at = jnp.where(end, 16, 4 * i + 2 * kind)
    layer = jnp.where(end, r - 24, r >> 3)
    values = jnp.where(end, weight(fine_row(c) - at, False), weight(fine_row(c) - at, kind == 1))
    blocks = [jnp.where(layer == l, values, 0.0) for l in range(3)]
    r, c = iota((32, 8), 0), iota((32, 8), 1)
    return jnp.concatenate(blocks + [jnp.where((c >> 1) == r - 27, 0.125, 0.0)], 1)


def window_matrix():
    r, c = iota((112, 96), 0), iota((112, 96), 1)
    l, kind, slot, i = r >> 5, (r & 31) >> 4, (r & 15) >> 2, r & 3
    at, k = c >> 5, c & 31
    body = (at == slot) & (k == 8 * l + 4 * kind + i)
    end = (kind == 0) & (i == 0) & (at == slot - 1) & (k == 24 + l)
    cells = (at == slot) & (k == 27 + i)
    return jnp.where(((r < 96) & (body | end)) | ((r >= 96) & cells), 1.0, 0.0)


def out_rows():
    r, c = iota((24, 24), 0), iota((24, 24), 1)
    merge = jnp.where(fine_row(c) == r, 1.0, 0.0)
    r, c = iota((24, 32), 0), iota((24, 32), 1)
    odd = c >= 16
    e = c & 15
    inside = (e >= 4) & (e <= jnp.where(odd, 7, 8))
    at = 4 * (e - 4) + jnp.where(odd, 2, 0)
    prolong = jnp.where(inside, weight(r - at, odd), 0.0)
    return jnp.concatenate([merge, prolong], 1)


def roll_x(v, step):
    lanes = v.shape[-1]
    return pltpu.roll(v.reshape(-1, lanes), step % lanes, 1).reshape(v.shape)


def roll_y(v, step):
    flat = v.reshape((-1,) + v.shape[-2:])
    return pltpu.roll(flat, step % v.shape[-2], 1).reshape(v.shape)


def forward(a, b, c):
    s = a + c
    return s + 4.0 * b, a - c, s - 2.0 * b


def backward(a, b, c, squared):
    s = a + c
    if squared:
        return s + b, 16.0 * a + 4.0 * c, s + b
    return s + b, 4.0 * a - 2.0 * c, s - b


def factors(cond, h):
    cells = cond.shape[0]
    out = []
    for l in range(3):
        rows = []
        for z in range(cells):
            for j in range(3):
                for i in range(3):
                    w = W[i] * W[j] * W[l]
                    rows.append(
                        cond[z] * (w * h * (EIG[i] + EIG[j] + EIG[l])) + w * REACTION * h**3
                    )
        out.append(jnp.stack(rows, 0).reshape((cells, 3, 3) + cond.shape[1:]))
    return out


def to_nodes(modes, squared=False):
    cells = modes[0].shape[0]
    row = iota(modes[0].shape[-2:], 0)
    low, mid, up = backward(*modes, squared)
    layers = [low[0]]
    for z in range(cells):
        layers.append(mid[z])
        layers.append(up[z] + low[z + 1] if z + 1 < cells else up[z])
    q = jnp.stack(layers, 0)
    low, mid, up = backward(q[:, 0], q[:, 1], q[:, 2], squared)
    even = low + jnp.where(row == 0, 0.0, roll_y(up, 1))
    q = jnp.stack([even, mid, up], 2)
    low, mid, up = backward(q[:, 0], q[:, 1], q[:, 2], squared)
    return low + roll_x(up, 1), mid


def apply_local(field, factor, ny):
    even, odd = field
    cells = factor[0].shape[0]
    row = iota(even.shape[-2:], 0)
    g = jnp.stack(forward(even, odd, roll_x(even, -1)), 0)
    low, mid, end = g[:, :, 0], g[:, :, 1], g[:, :, 2]
    up = jnp.where(row == ny - 1, end, roll_y(low, -1))
    y = jnp.stack(forward(low, mid, up), 0)
    parts = [jnp.stack([y[:, :, 2 * z + a] for z in range(cells)], 0) for a in range(3)]
    modes = forward(*parts)
    return to_nodes([m * f for m, f in zip(modes, factor)])


def window_nodes(modes, squared=False):
    cells = modes[0].shape[0]
    low, mid, up = backward(*modes, squared)
    layers = []
    for z in range(cells):
        layers += [low[z] + up[z - 1], mid[z]]
    q = jnp.stack(layers, 0)
    low, mid, up = backward(q[:, 0], q[:, 1], q[:, 2], squared)
    q = jnp.stack([low + roll_y(up, 1), mid], 2)
    low, mid, up = backward(q[:, 0], q[:, 1], q[:, 2], squared)
    return low + roll_x(up, 1), mid


def apply_window(field, factor):
    even, odd = field
    cells = factor[0].shape[0]
    g = jnp.stack(forward(even, odd, roll_x(even, -1)), 0)
    low, mid = g[:, :, 0], g[:, :, 1]
    y = jnp.stack(forward(low, mid, roll_y(low, -1)), 0)
    parts = [
        jnp.stack([y[:, :, (2 * z + a) % (2 * cells)] for z in range(cells)], 0)
        for a in range(3)
    ]
    modes = forward(*parts)
    return window_nodes([m * f for m, f in zip(modes, factor)])


def exchange(fields, phase, ny, bufs, beside=None):
    zs, zr, ys, yr, cs, cr, send_sem, recv_sem = bufs
    flat = [part for field in fields for part in field]
    count = len(flat)
    layers = flat[0].shape[0]
    last = layers - 1
    row = iota(flat[0].shape[-2:], 0)
    for f, part in enumerate(flat):
        zs[phase, 0, f] = part[last]
        zs[phase, 1, f] = part[0]
        for l in range(layers):
            ys[phase, 0, f, l : l + 1] = part[l, 2, ny - 1 : ny]
            ys[phase, 1, f, l : l + 1] = part[l, 0, 0:1]
        cs[phase, 0, f : f + 1] = part[last, 2, ny - 1 : ny]
        cs[phase, 1, f : f + 1] = part[0, 2, ny - 1 : ny]
        cs[phase, 2, f : f + 1] = part[last, 0, 0:1]
        cs[phase, 3, f : f + 1] = part[0, 0, 0:1]
    gy, gz = lax.axis_size("gy"), lax.axis_size("gz")
    iy, iz = lax.axis_index("gy"), lax.axis_index("gz")
    copies = []
    for k in (2, 3, 0, 1, 4, 5, 6, 7):
        dy, dz = STEPS[k]
        if k < 2:
            src, dst = ys.at[phase, k, pl.ds(0, count)], yr.at[phase, k, pl.ds(0, count)]
        elif k < 4:
            src, dst = zs.at[phase, k - 2, pl.ds(0, count)], zr.at[phase, k - 2, pl.ds(0, count)]
        else:
            src, dst = cs.at[phase, k - 4], cr.at[phase, k - 4]
        copy = pltpu.make_async_remote_copy(
            src_ref=src,
            dst_ref=dst,
            send_sem=send_sem.at[phase, k],
            recv_sem=recv_sem.at[phase, k],
            device_id={"gy": lax.rem(iy + dy + gy, gy), "gz": lax.rem(iz + dz + gz, gz)},
            device_id_type=MESH,
        )
        copy.start()
        copies.append(copy)
    if beside is not None:
        beside()
    for copy in copies:
        copy.wait_recv()
    out = []
    for f, part in enumerate(flat):
        done = []
        for l in range(layers):
            first = yr[phase, 0, f, l : l + 1]
            end = yr[phase, 1, f, l : l + 1]
            if l == last:
                first = first + cr[phase, 1, f : f + 1]
                end = end + cr[phase, 3, f : f + 1]
            if l == 0:
                first = first + cr[phase, 0, f : f + 1]
                end = end + cr[phase, 2, f : f + 1]
            low = part[l, 0] + jnp.where(row == 0, first, 0.0)
            layer = jnp.stack([low, part[l, 1], part[l, 2] + end], 0)
            if l == 0:
                layer = layer + zr[phase, 0, f]
            if l == last:
                layer = layer + zr[phase, 1, f]
            done.append(layer)
        out.append(jnp.stack(done, 0))
    return [(out[2 * i], out[2 * i + 1]) for i in range(len(fields))], copies


def inverse(diagonal, ny):
    row = iota(diagonal.shape[-2:], 0)
    whole = jnp.where(row < ny, 1.0 / diagonal[:, 0:2], 0.0)
    end = jnp.where(row == ny - 1, 1.0 / diagonal[:, 2:3], 0.0)
    return jnp.concatenate([whole, end], 1)


def chebyshev(right, scaled, operate, degree):
    centre = 0.5 * (UPPER + LOWER)
    half = 0.5 * (UPPER - LOWER)
    sharp = centre / half
    f = 1.0 / sharp
    update = [s * r * (1.0 / centre) for s, r in zip(scaled, right)]
    total = update
    for k in range(1, degree):
        image = operate(total, k)
        g = 1.0 / (2.0 * sharp - f)
        update = [
            (g * f) * u + (2.0 * g / half) * (s * (r - a))
            for u, s, r, a in zip(update, scaled, right, image)
        ]
        total = [t + u for t, u in zip(total, update)]
        f = g
    return total


def kernel(load_ref, cond_ref, out_ref, line, cells, cell_out, zs, zr, ys, yr, cs, cr,
           send_sem, recv_sem, x_send, x_recv, matrix_x, matrix_out,
           packets, w_send, w_recv):
    gx, gy, gz = lax.axis_size("gx"), lax.axis_size("gy"), lax.axis_size("gz")
    ix, iy, iz = lax.axis_index("gx"), lax.axis_index("gy"), lax.axis_index("gz")
    lanes = 64 * gx
    bufs = (zs, zr, ys, yr, cs, cr, send_sem, recv_sem)
    barrier = pltpu.get_barrier_semaphore()
    wide_z = packets.shape[0]
    own_z = wide_z // 2
    slots = [
        (z, y) for z in range(wide_z) for y in range(3) if (z, y) != (own_z, 1)
    ]

    def holder(slot):
        return {
            "gy": lax.rem(iy + 1 - slot[1] + gy, gy),
            "gz": lax.rem(iz + own_z - slot[0] + gz, gz),
        }

    for slot in slots:
        pl.semaphore_signal(barrier, inc=1, device_id=holder(slot), device_id_type=MESH)
    for d in range(1, gx):
        pl.semaphore_signal(
            barrier, inc=1, device_id={"gx": lax.rem(ix + d, gx)}, device_id_type=MESH
        )
    cell_out[...] = jnp.zeros(cell_out.shape, jnp.float32)
    cell_out[:, :, 0:64] = cond_ref[...]
    pl.semaphore_wait(barrier, len(slots) + gx - 1)
    started = []
    arrivals = []
    for d in range(1, gx):
        for k, (src, dst) in enumerate(((load_ref, line), (cell_out, cells))):
            copy = pltpu.make_async_remote_copy(
                src_ref=src,
                dst_ref=dst.at[gx - d - 1],
                send_sem=x_send.at[k, d - 1],
                recv_sem=x_recv.at[k, gx - d - 1],
                device_id={"gx": lax.rem(ix + d, gx)},
                device_id_type=MESH,
            )
            copy.start()
            arrivals.append(copy)
    split_x, place = split_matrix(lanes), place_matrix(lanes)
    for copy in arrivals:
        copy.wait_recv()
    started += arrivals

    def rows(ref):
        parts = []
        for z in range(5):
            parts.append(ref[z, pl.ds(0, 8, stride=2), :])
            parts.append(ref[z, pl.ds(1, 8, stride=2), :])
            parts.append(jnp.broadcast_to(ref[z, 16:17, :], (8, 128)))
        return jnp.concatenate(parts, 0)

    joined = jnp.concatenate(
        [rows(load_ref)] + [rows(line.at[d]) for d in range(gx - 1)], 1
    )
    loads = dot_right(joined, split_x)
    load = (loads[:, :lanes].reshape(5, 3, 8, lanes), loads[:, lanes:].reshape(5, 3, 8, lanes))
    joined = jnp.concatenate(
        [cell_out[...].reshape(16, 128)] + [cells[d].reshape(16, 128) for d in range(gx - 1)], 1
    )
    conds = dot_right(joined, place)
    cond = conds[:, :lanes].reshape(2, 8, lanes)
    pair = conds[:8, lanes:] + conds[8:, lanes:]

    fine = factors(cond, 1.0)

    def fill():
        matrix_x[...] = restrict_matrix(lanes)
        matrix_out[...] = out_matrix(lanes)

    (right, diagonal), copies = exchange([load, to_nodes(fine, True)], 0, 8, bufs, fill)
    started += copies

    def operate(field, k):
        (image,), copies = exchange([apply_local(field, fine, 8)], k, 8, bufs)
        started.extend(copies)
        return image

    smooth = chebyshev(right, [inverse(d, 8) for d in diagonal], operate, DEG1)
    image = apply_local(smooth, fine, 8)
    part = [
        jnp.concatenate([(b - a).reshape(5, 24, lanes) for b, a in zip(load, image)], 2)
    ][0]
    f0, f1, f2, f3, f4 = (part[z] for z in range(5))
    three = jnp.concatenate(
        [
            f0 + 0.375 * f1 - 0.125 * f3,
            0.75 * f1 + f2 + 0.75 * f3,
            -0.125 * f1 + 0.375 * f3 + f4,
        ],
        0,
    )
    three = dot_right(three, matrix_x[...])
    packets[own_z, 1] = dot_left(packet_matrix(), jnp.concatenate([three, pair], 0))
    copies = []
    for slot in slots:
        copy = pltpu.make_async_remote_copy(
            src_ref=packets.at[own_z, 1],
            dst_ref=packets.at[slot],
            send_sem=w_send.at[slot],
            recv_sem=w_recv.at[slot],
            device_id=holder(slot),
            device_id_type=MESH,
        )
        copy.start()
        copies.append(copy)
    started += copies
    own = jnp.concatenate([s.reshape(120, lanes) for s in smooth], 1)
    own = dot_right(own, matrix_out[:, :128])
    gather = window_matrix()
    for copy in copies:
        copy.wait_recv()
    tall = [
        jnp.concatenate([packets[z, y] for y in range(3)], 0) for z in range(wide_z)
    ]
    tall = dot_left(gather, jnp.concatenate(tall, 1))
    tall = [tall[:, z * lanes : (z + 1) * lanes] for z in range(wide_z)]
    layers = []
    for z in range(wide_z):
        layers += [tall[z][0:32] + tall[z - 1][64:96], tall[z][32:64]]
    packed = jnp.stack(layers, 0).reshape(2 * wide_z, 2, 16, lanes)
    turned = roll_x(packed, lanes // 2)
    first = iota(packed.shape[-2:], 1) < lanes // 2
    right = (jnp.where(first, packed, turned), jnp.where(first, turned, packed))
    coarse = factors(jnp.stack([t[96:112] for t in tall], 0), 2.0)
    diagonal = window_nodes(coarse, True)
    correction = chebyshev(
        right, [1.0 / d for d in diagonal], lambda v, k: apply_window(v, coarse), DEG2
    )
    c0, c1, c2 = (
        jnp.concatenate([v[(2 * own_z + l) % (2 * wide_z)].reshape(32, lanes) for v in correction], 1)
        for l in range(3)
    )
    five = jnp.concatenate(
        [
            c0,
            0.375 * c0 + 0.75 * c1 - 0.125 * c2,
            c1,
            -0.125 * c0 + 0.75 * c1 + 0.375 * c2,
            c2,
        ],
        0,
    )
    five = dot_right(five, matrix_out[:, 128:])
    tall = jnp.concatenate(
        [
            jnp.concatenate([v[n * z : n * z + n] for z in range(5)], 1)
            for v, n in ((own, 24), (five, 32))
        ],
        0,
    )
    result = dot_left(out_rows(), tall)
    for z in range(5):
        out_ref[z] = result[0:17, 128 * z : 128 * z + 128]
    for copy in started:
        copy.wait_send()


def solution(mesh):
    gx = mesh.shape["gx"]
    lanes = 64 * gx
    phases = DEG1
    wide_z = min(mesh.shape["gz"], 9)

    def step(element_load, conductivity):
        vmem = pl.BlockSpec(memory_space=pltpu.VMEM)
        f32 = jnp.float32
        return pl.pallas_call(
            kernel,
            out_shape=jax.ShapeDtypeStruct(element_load.shape, f32),
            in_specs=[vmem, vmem],
            out_specs=vmem,
            scratch_shapes=[
                pltpu.VMEM((gx - 1,) + element_load.shape, f32),
                pltpu.VMEM((gx - 1, 2, 8, 128), f32),
                pltpu.VMEM((2, 8, 128), f32),
                pltpu.VMEM((phases, 2, 4, 3, 8, lanes), f32),
                pltpu.VMEM((phases, 2, 4, 3, 8, lanes), f32),
                pltpu.VMEM((phases, 2, 4, 8, lanes), f32),
                pltpu.VMEM((phases, 2, 4, 8, lanes), f32),
                pltpu.VMEM((phases, 4, 8, lanes), f32),
                pltpu.VMEM((phases, 4, 8, lanes), f32),
                pltpu.SemaphoreType.DMA((phases, 8)),
                pltpu.SemaphoreType.DMA((phases, 8)),
                pltpu.SemaphoreType.DMA((2, gx - 1)),
                pltpu.SemaphoreType.DMA((2, gx - 1)),
                pltpu.VMEM((2 * lanes, lanes), jnp.bfloat16),
                pltpu.VMEM((2 * lanes, 256), jnp.bfloat16),
                pltpu.VMEM((wide_z, 3, 32, lanes), f32),
                pltpu.SemaphoreType.DMA((wide_z, 3)),
                pltpu.SemaphoreType.DMA((wide_z, 3)),
            ],
            compiler_params=pltpu.CompilerParams(
                collective_id=0, has_side_effects=True, vmem_limit_bytes=48 * 1024 * 1024
            ),
        )(element_load, conductivity)

    spec = P("gz", "gy", "gx")
    return jax.shard_map(
        step, mesh=mesh, in_specs=(spec, spec), out_specs=spec, check_vma=False
    )
```

```python
import functools

import jax
import jax.numpy as jnp
from jax import lax
from jax.experimental import pallas as pl
from jax.experimental.pallas import tpu as pltpu
from jax.sharding import PartitionSpec as P

DEG1 = 3
DEG2 = 4
REACTION = 0.05
LOWER = 0.25
UPPER = 2.5
EIG = (0.0, 12.0, 60.0)
W = (1.0 / 36.0, 1.0 / 12.0, 1.0 / 45.0)
MESH = pl.DeviceIdType.MESH
STEPS = ((1, 0), (-1, 0), (0, 1), (0, -1), (1, 1), (1, -1), (-1, 1), (-1, -1))


def iota(shape, dim):
    return lax.broadcasted_iota(jnp.int32, shape, dim)


def pieces(v):
    high = v.astype(jnp.bfloat16).astype(jnp.float32)
    rest = v - high
    mid = rest.astype(jnp.bfloat16).astype(jnp.float32)
    return [high, mid, rest - mid]


def dot_right(v, matrix):
    n = v.shape[0]
    tall = jnp.concatenate(pieces(v), 0).astype(jnp.bfloat16)
    out = jnp.dot(tall, matrix, preferred_element_type=jnp.float32)
    return out[2 * n :] + out[n : 2 * n] + out[:n]


def dot_left(matrix, v):
    tall = jnp.concatenate(pieces(v), 0).astype(jnp.bfloat16)
    wide = jnp.concatenate([matrix] * 3, 1).astype(jnp.bfloat16)
    return jnp.dot(wide, tall, preferred_element_type=jnp.float32)


def weight(d, odd):
    a = jnp.abs(d)
    even_w = jnp.where(a == 0, 1.0, jnp.where(a == 1, 0.375, jnp.where(a == 3, -0.125, 0.0)))
    odd_w = jnp.where(a == 0, 1.0, jnp.where(a == 1, 0.75, 0.0))
    return jnp.where(odd, odd_w, even_w)


def wrapped(d, period):
    d = jnp.where(d > period // 2, d - period, d)
    return jnp.where(d < -(period // 2), d + period, d)


def bits(n):
    return n.bit_length() - 1


def split_matrix(lanes):
    n = 2 * lanes
    r, c = iota((n, n), 0), iota((n, n), 1)
    return jnp.where(r == 2 * (c & (lanes - 1)) + (c >> bits(lanes)), 1.0, 0.0).astype(jnp.bfloat16)


def place_matrix(lanes):
    r, c = iota((2 * lanes, 3 * lanes), 0), iota((2 * lanes, 3 * lanes), 1)
    layer, e = (r >> 6) & 1, ((r >> 7) << 6) + (r & 63)
    block, at = c >> bits(lanes), c & (lanes - 1)
    hit = ((block == layer) & (e == at)) | ((block == 2) & ((e >> 1) == (at & (lanes // 2 - 1))))
    return jnp.where(hit, 1.0, 0.0).astype(jnp.bfloat16)


def restrict_matrix(lanes):
    n = 2 * lanes
    r, c = iota((n, lanes), 0), iota((n, lanes), 1)
    node = 2 * (r & (lanes - 1)) + (r >> bits(lanes))
    cp, m = c >> bits(lanes // 2), c & (lanes // 2 - 1)
    return weight(wrapped(node - 4 * m - 2 * cp, n), cp == 1).astype(jnp.bfloat16)


def out_matrix(lanes):
    n = 2 * lanes
    r, c = iota((n, 128), 0), iota((n, 128), 1)
    m, cp = r & (lanes - 1), r >> bits(lanes)
    merge = jnp.where(2 * m + cp == c, 1.0, 0.0)
    prolong = jnp.where(
        m < lanes // 2, weight(wrapped(c - 4 * m - 2 * cp, n), cp == 1), 0.0
    )
    return jnp.concatenate([merge, prolong], 1).astype(jnp.bfloat16)


def fine_row(r):
    kind, i = r >> 3, r & 7
    return jnp.where(kind == 2, jnp.where(i == 7, 16, 1000), 2 * i + kind)


def packet_matrix():
    r, c = iota((32, 24), 0), iota((32, 24), 1)
    kind, i = (r & 7) >> 2, r & 3
    end = r >= 24
    at = jnp.where(end, 16, 4 * i + 2 * kind)
    layer = jnp.where(end, r - 24, r >> 3)
    values = jnp.where(end, weight(fine_row(c) - at, False), weight(fine_row(c) - at, kind == 1))
    blocks = [jnp.where(layer == l, values, 0.0) for l in range(3)]
    r, c = iota((32, 8), 0), iota((32, 8), 1)
    return jnp.concatenate(blocks + [jnp.where((c >> 1) == r - 27, 0.125, 0.0)], 1)


def window_matrix():
    r, c = iota((112, 96), 0), iota((112, 96), 1)
    l, kind, slot, i = r >> 5, (r & 31) >> 4, (r & 15) >> 2, r & 3
    at, k = c >> 5, c & 31
    body = (at == slot) & (k == 8 * l + 4 * kind + i)
    end = (kind == 0) & (i == 0) & (at == slot - 1) & (k == 24 + l)
    cells = (at == slot) & (k == 27 + i)
    return jnp.where(((r < 96) & (body | end)) | ((r >= 96) & cells), 1.0, 0.0)


def out_rows():
    r, c = iota((24, 24), 0), iota((24, 24), 1)
    merge = jnp.where(fine_row(c) == r, 1.0, 0.0)
    r, c = iota((24, 32), 0), iota((24, 32), 1)
    odd = c >= 16
    e = c & 15
    inside = (e >= 4) & (e <= jnp.where(odd, 7, 8))
    at = 4 * (e - 4) + jnp.where(odd, 2, 0)
    prolong = jnp.where(inside, weight(r - at, odd), 0.0)
    return jnp.concatenate([merge, prolong], 1)


def roll_x(v, step):
    lanes = v.shape[-1]
    return pltpu.roll(v.reshape(-1, lanes), step % lanes, 1).reshape(v.shape)


def roll_y(v, step):
    flat = v.reshape((-1,) + v.shape[-2:])
    return pltpu.roll(flat, step % v.shape[-2], 1).reshape(v.shape)


def forward(a, b, c):
    s = a + c
    return s + 4.0 * b, a - c, s - 2.0 * b


def backward(a, b, c, squared):
    s = a + c
    if squared:
        return s + b, 16.0 * a + 4.0 * c, s + b
    return s + b, 4.0 * a - 2.0 * c, s - b


def factors(cond, h):
    cells = cond.shape[0]
    out = []
    for l in range(3):
        rows = []
        for z in range(cells):
            for j in range(3):
                for i in range(3):
                    w = W[i] * W[j] * W[l]
                    rows.append(
                        cond[z] * (w * h * (EIG[i] + EIG[j] + EIG[l])) + w * REACTION * h**3
                    )
        out.append(jnp.stack(rows, 0).reshape((cells, 3, 3) + cond.shape[1:]))
    return out


def to_nodes(modes, squared=False):
    cells = modes[0].shape[0]
    row = iota(modes[0].shape[-2:], 0)
    low, mid, up = backward(*modes, squared)
    layers = [low[0]]
    for z in range(cells):
        layers.append(mid[z])
        layers.append(up[z] + low[z + 1] if z + 1 < cells else up[z])
    q = jnp.stack(layers, 0)
    low, mid, up = backward(q[:, 0], q[:, 1], q[:, 2], squared)
    even = low + jnp.where(row == 0, 0.0, roll_y(up, 1))
    q = jnp.stack([even, mid, up], 2)
    low, mid, up = backward(q[:, 0], q[:, 1], q[:, 2], squared)
    return low + roll_x(up, 1), mid


def apply_local(field, factor, ny):
    even, odd = field
    cells = factor[0].shape[0]
    row = iota(even.shape[-2:], 0)
    g = jnp.stack(forward(even, odd, roll_x(even, -1)), 0)
    low, mid, end = g[:, :, 0], g[:, :, 1], g[:, :, 2]
    up = jnp.where(row == ny - 1, end, roll_y(low, -1))
    y = jnp.stack(forward(low, mid, up), 0)
    parts = [jnp.stack([y[:, :, 2 * z + a] for z in range(cells)], 0) for a in range(3)]
    modes = forward(*parts)
    return to_nodes([m * f for m, f in zip(modes, factor)])


def window_nodes(modes, squared=False):
    cells = modes[0].shape[0]
    low, mid, up = backward(*modes, squared)
    layers = []
    for z in range(cells):
        layers += [low[z] + up[z - 1], mid[z]]
    q = jnp.stack(layers, 0)
    low, mid, up = backward(q[:, 0], q[:, 1], q[:, 2], squared)
    q = jnp.stack([low + roll_y(up, 1), mid], 2)
    low, mid, up = backward(q[:, 0], q[:, 1], q[:, 2], squared)
    return low + roll_x(up, 1), mid


def apply_window(field, factor):
    even, odd = field
    cells = factor[0].shape[0]
    g = jnp.stack(forward(even, odd, roll_x(even, -1)), 0)
    low, mid = g[:, :, 0], g[:, :, 1]
    y = jnp.stack(forward(low, mid, roll_y(low, -1)), 0)
    parts = [
        jnp.stack([y[:, :, (2 * z + a) % (2 * cells)] for z in range(cells)], 0)
        for a in range(3)
    ]
    modes = forward(*parts)
    return window_nodes([m * f for m, f in zip(modes, factor)])


def exchange(fields, phase, ny, bufs, beside=None):
    zs, zr, ys, yr, cs, cr, send_sem, recv_sem = bufs
    flat = [part for field in fields for part in field]
    count = len(flat)
    layers = flat[0].shape[0]
    last = layers - 1
    row = iota(flat[0].shape[-2:], 0)
    for f, part in enumerate(flat):
        zs[phase, 0, f] = part[last]
        zs[phase, 1, f] = part[0]
        for l in range(layers):
            ys[phase, 0, f, l : l + 1] = part[l, 2, ny - 1 : ny]
            ys[phase, 1, f, l : l + 1] = part[l, 0, 0:1]
        cs[phase, 0, f : f + 1] = part[last, 2, ny - 1 : ny]
        cs[phase, 1, f : f + 1] = part[0, 2, ny - 1 : ny]
        cs[phase, 2, f : f + 1] = part[last, 0, 0:1]
        cs[phase, 3, f : f + 1] = part[0, 0, 0:1]
    gy, gz = lax.axis_size("gy"), lax.axis_size("gz")
    iy, iz = lax.axis_index("gy"), lax.axis_index("gz")
    copies = []
    for k in (2, 3, 0, 1, 4, 5, 6, 7):
        dy, dz = STEPS[k]
        if k < 2:
            src, dst = ys.at[phase, k, pl.ds(0, count)], yr.at[phase, k, pl.ds(0, count)]
        elif k < 4:
            src, dst = zs.at[phase, k - 2, pl.ds(0, count)], zr.at[phase, k - 2, pl.ds(0, count)]
        else:
            src, dst = cs.at[phase, k - 4], cr.at[phase, k - 4]
        copy = pltpu.make_async_remote_copy(
            src_ref=src,
            dst_ref=dst,
            send_sem=send_sem.at[phase, k],
            recv_sem=recv_sem.at[phase, k],
            device_id={"gy": lax.rem(iy + dy + gy, gy), "gz": lax.rem(iz + dz + gz, gz)},
            device_id_type=MESH,
        )
        copy.start()
        copies.append(copy)
    if beside is not None:
        beside()
    for copy in copies:
        copy.wait_recv()
    out = []
    for f, part in enumerate(flat):
        done = []
        for l in range(layers):
            first = yr[phase, 0, f, l : l + 1]
            end = yr[phase, 1, f, l : l + 1]
            if l == last:
                first = first + cr[phase, 1, f : f + 1]
                end = end + cr[phase, 3, f : f + 1]
            if l == 0:
                first = first + cr[phase, 0, f : f + 1]
                end = end + cr[phase, 2, f : f + 1]
            low = part[l, 0] + jnp.where(row == 0, first, 0.0)
            layer = jnp.stack([low, part[l, 1], part[l, 2] + end], 0)
            if l == 0:
                layer = layer + zr[phase, 0, f]
            if l == last:
                layer = layer + zr[phase, 1, f]
            done.append(layer)
        out.append(jnp.stack(done, 0))
    return [(out[2 * i], out[2 * i + 1]) for i in range(len(fields))], copies


def fine_diagonal(cells, below, above):
    row = iota(cells.shape[-2:], 0)
    mass, stiff = (4.0 / 30.0, 16.0 / 30.0), (7.0 / 3.0, 16.0 / 3.0)
    out = []
    for x in range(2):
        v, lo, hi = cells, below, above
        if x == 0:
            v, lo, hi = (t + roll_x(t, 1) for t in (v, lo, hi))
        rows = ((v + jnp.where(row == 0, lo, roll_y(v, 1)), 0), (v, 1), (v + hi, 0))
        parts = []
        for z in range(5):
            for t, y in rows:
                near = t[z // 2 + 1] if z % 2 else t[z // 2] + t[z // 2 + 1]
                k = (x, y, z % 2)
                m = [mass[i] for i in k]
                w = [stiff[i] for i in k]
                share = w[0] * m[1] * m[2] + m[0] * w[1] * m[2] + m[0] * m[1] * w[2]
                count = 2 ** (3 - sum(k))
                parts.append(near * share + REACTION * m[0] * m[1] * m[2] * count)
        out.append(jnp.stack(parts, 0).reshape((5, 3) + cells.shape[1:]))
    return out


def inverse(diagonal, ny):
    row = iota(diagonal.shape[-2:], 0)
    whole = jnp.where(row < ny, 1.0 / diagonal[:, 0:2], 0.0)
    end = jnp.where(row == ny - 1, 1.0 / diagonal[:, 2:3], 0.0)
    return jnp.concatenate([whole, end], 1)


def chebyshev(right, scaled, operate, degree):
    centre = 0.5 * (UPPER + LOWER)
    half = 0.5 * (UPPER - LOWER)
    sharp = centre / half
    f = 1.0 / sharp
    update = [s * r * (1.0 / centre) for s, r in zip(scaled, right)]
    total = update
    for k in range(1, degree):
        image = operate(total, k)
        g = 1.0 / (2.0 * sharp - f)
        update = [
            (g * f) * u + (2.0 * g / half) * (s * (r - a))
            for u, s, r, a in zip(update, scaled, right, image)
        ]
        total = [t + u for t, u in zip(total, update)]
        f = g
    return total


def kernel(load_ref, cond_ref, out_ref, line, cells, cell_out, zs, zr, ys, yr, cs, cr,
           send_sem, recv_sem, x_send, x_recv, matrix_x, matrix_out,
           packets, w_send, w_recv, near, far, n_send, n_recv, summed):
    gx, gy, gz = lax.axis_size("gx"), lax.axis_size("gy"), lax.axis_size("gz")
    ix, iy, iz = lax.axis_index("gx"), lax.axis_index("gy"), lax.axis_index("gz")
    lanes = 64 * gx
    bufs = (zs, zr, ys, yr, cs, cr, send_sem, recv_sem)
    barrier = pltpu.get_barrier_semaphore()
    wide_z = packets.shape[0]
    own_z = wide_z // 2
    slots = [
        (z, y) for z in range(wide_z) for y in range(3) if (z, y) != (own_z, 1)
    ]

    def holder(slot):
        return {
            "gy": lax.rem(iy + 1 - slot[1] + gy, gy),
            "gz": lax.rem(iz + own_z - slot[0] + gz, gz),
        }

    def beside(step, d):
        return {
            "gx": lax.rem(ix + d, gx),
            "gy": lax.rem(iy + step[0] + gy, gy),
            "gz": lax.rem(iz + step[1] + gz, gz),
        }

    for slot in slots:
        pl.semaphore_signal(barrier, inc=1, device_id=holder(slot), device_id_type=MESH)
    for step in STEPS:
        for d in range(1, gx):
            pl.semaphore_signal(barrier, inc=1, device_id=beside(step, d), device_id_type=MESH)
    for d in range(1, gx):
        pl.semaphore_signal(
            barrier, inc=1, device_id={"gx": lax.rem(ix + d, gx)}, device_id_type=MESH
        )
    cell_out[:, 0:64] = cond_ref[0]
    cell_out[:, 64:128] = cond_ref[1]
    for k, (dy, dz) in enumerate(STEPS):
        y, z = (16 if dy == 1 else 0), (4 if dz == 1 else 0)
        if dy == 0:
            near[k, 0:17] = load_ref[z]
            near[k, 24:32] = cell_out[...]
        else:
            for l in range(5) if dz == 0 else (0,):
                near[k, l : l + 1] = load_ref[l if dz == 0 else z, y : y + 1]
            near[k, 5:6] = cell_out[7:8] if dy == 1 else cell_out[0:1]
    pl.semaphore_wait(barrier, len(slots) + 9 * (gx - 1))
    started = []
    arrivals = []
    for d in range(1, gx):
        for k, (src, dst) in enumerate(((load_ref, line), (cell_out, cells))):
            copy = pltpu.make_async_remote_copy(
                src_ref=src,
                dst_ref=dst.at[gx - d - 1],
                send_sem=x_send.at[k, d - 1],
                recv_sem=x_recv.at[k, gx - d - 1],
                device_id={"gx": lax.rem(ix + d, gx)},
                device_id_type=MESH,
            )
            copy.start()
            arrivals.append(copy)
    for k in (4, 5, 6, 7, 2, 3, 0, 1):
        count = 32 if STEPS[k][0] == 0 else 8
        for d in range(gx):
            copy = pltpu.make_async_remote_copy(
                src_ref=near.at[k, pl.ds(0, count)],
                dst_ref=far.at[k, (gx - d) % gx, pl.ds(0, count)],
                send_sem=n_send.at[k, d],
                recv_sem=n_recv.at[k, (gx - d) % gx],
                device_id=beside(STEPS[k], d),
                device_id_type=MESH,
            )
            copy.start()
            arrivals.append(copy)
    matrix_x[...] = restrict_matrix(lanes)
    matrix_out[...] = out_matrix(lanes)
    split_x, place = split_matrix(lanes), place_matrix(lanes)
    for copy in arrivals:
        copy.wait_recv()
    started += arrivals

    def rows(ref):
        parts = []
        for z in range(5):
            parts.append(ref[z, pl.ds(0, 8, stride=2), :])
            parts.append(ref[z, pl.ds(1, 8, stride=2), :])
            parts.append(jnp.broadcast_to(ref[z, 16:17, :], (8, 128)))
        return jnp.concatenate(parts, 0)

    bricks = [load_ref] + [line.at[d] for d in range(gx - 1)]
    for g, brick in enumerate(bricks):
        for z in range(5):
            v = brick[z]
            first, end = far[0, g, z : z + 1], far[1, g, z : z + 1]
            if z == 0:
                v = v + far[2, g, 0:17]
                first, end = first + far[4, g, 0:1], end + far[6, g, 0:1]
            if z == 4:
                v = v + far[3, g, 0:17]
                first, end = first + far[5, g, 0:1], end + far[7, g, 0:1]
            summed[g, z] = v
            summed[g, z, 0:1] = v[0:1] + first
            summed[g, z, 16:17] = v[16:17] + end
    joined = jnp.concatenate(
        [
            jnp.concatenate([rows(b) for b in bricks], 1),
            jnp.concatenate([rows(summed.at[g]) for g in range(gx)], 1),
        ],
        0,
    )
    loads = dot_right(joined, split_x).reshape(2, 5, 3, 8, 2 * lanes)
    load, right = (
        (loads[i, :, :, :, :lanes], loads[i, :, :, :, lanes:]) for i in range(2)
    )
    owned = [cell_out] + [cells.at[d] for d in range(gx - 1)]
    joined = jnp.concatenate(
        [
            jnp.concatenate(
                [owned[g][...], far[2, g, 24:32], far[3, g, 24:32]]
                + [far[k, g, 0:8] for k in (0, 1, 4, 5, 6, 7)],
                0,
            )
            for g in range(gx)
        ],
        1,
    )
    conds = dot_right(joined, place)

    def one(at, layer):
        row = conds[at + 5 : at + 6, layer * lanes : (layer + 1) * lanes]
        return jnp.broadcast_to(row, (8, lanes))

    cond = jnp.stack([conds[0:8, :lanes], conds[0:8, lanes : 2 * lanes]], 0)
    around = jnp.stack(
        [conds[8:16, lanes : 2 * lanes], cond[0], cond[1], conds[16:24, :lanes]], 0
    )
    below = jnp.stack([one(40, 1), one(24, 0), one(24, 1), one(48, 0)], 0)
    above = jnp.stack([one(56, 1), one(32, 0), one(32, 1), one(64, 0)], 0)
    pair = conds[0:8, 2 * lanes :]
    fine = factors(cond, 1.0)
    diagonal = fine_diagonal(around, below, above)

    def operate(field, k):
        (image,), copies = exchange([apply_local(field, fine, 8)], k - 1, 8, bufs)
        started.extend(copies)
        return image

    smooth = chebyshev(right, [inverse(d, 8) for d in diagonal], operate, DEG1)
    image = apply_local(smooth, fine, 8)
    part = [
        jnp.concatenate([(b - a).reshape(5, 24, lanes) for b, a in zip(load, image)], 2)
    ][0]
    f0, f1, f2, f3, f4 = (part[z] for z in range(5))
    three = jnp.concatenate(
        [
            f0 + 0.375 * f1 - 0.125 * f3,
            0.75 * f1 + f2 + 0.75 * f3,
            -0.125 * f1 + 0.375 * f3 + f4,
        ],
        0,
    )
    three = dot_right(three, matrix_x[...])
    packets[own_z, 1] = dot_left(packet_matrix(), jnp.concatenate([three, pair], 0))
    copies = []
    for slot in slots:
        copy = pltpu.make_async_remote_copy(
            src_ref=packets.at[own_z, 1],
            dst_ref=packets.at[slot],
            send_sem=w_send.at[slot],
            recv_sem=w_recv.at[slot],
            device_id=holder(slot),
            device_id_type=MESH,
        )
        copy.start()
        copies.append(copy)
    started += copies
    own = jnp.concatenate([s.reshape(120, lanes) for s in smooth], 1)
    own = dot_right(own, matrix_out[:, :128])
    gather = window_matrix()
    for copy in copies:
        copy.wait_recv()
    tall = [
        jnp.concatenate([packets[z, y] for y in range(3)], 0) for z in range(wide_z)
    ]
    tall = dot_left(gather, jnp.concatenate(tall, 1))
    tall = [tall[:, z * lanes : (z + 1) * lanes] for z in range(wide_z)]
    layers = []
    for z in range(wide_z):
        layers += [tall[z][0:32] + tall[z - 1][64:96], tall[z][32:64]]
    packed = jnp.stack(layers, 0).reshape(2 * wide_z, 2, 16, lanes)
    turned = roll_x(packed, lanes // 2)
    first = iota(packed.shape[-2:], 1) < lanes // 2
    right = (jnp.where(first, packed, turned), jnp.where(first, turned, packed))
    coarse = factors(jnp.stack([t[96:112] for t in tall], 0), 2.0)
    diagonal = window_nodes(coarse, True)
    correction = chebyshev(
        right, [1.0 / d for d in diagonal], lambda v, k: apply_window(v, coarse), DEG2
    )
    c0, c1, c2 = (
        jnp.concatenate([v[(2 * own_z + l) % (2 * wide_z)].reshape(32, lanes) for v in correction], 1)
        for l in range(3)
    )
    five = jnp.concatenate(
        [
            c0,
            0.375 * c0 + 0.75 * c1 - 0.125 * c2,
            c1,
            -0.125 * c0 + 0.75 * c1 + 0.375 * c2,
            c2,
        ],
        0,
    )
    five = dot_right(five, matrix_out[:, 128:])
    tall = jnp.concatenate(
        [
            jnp.concatenate([v[n * z : n * z + n] for z in range(5)], 1)
            for v, n in ((own, 24), (five, 32))
        ],
        0,
    )
    result = dot_left(out_rows(), tall)
    for z in range(5):
        out_ref[z] = result[0:17, 128 * z : 128 * z + 128]
    for copy in started:
        copy.wait_send()


def solution(mesh):
    gx = mesh.shape["gx"]
    lanes = 64 * gx
    phases = DEG1 - 1
    wide_z = min(mesh.shape["gz"], 9)

    def step(element_load, conductivity):
        vmem = pl.BlockSpec(memory_space=pltpu.VMEM)
        f32 = jnp.float32
        return pl.pallas_call(
            kernel,
            out_shape=jax.ShapeDtypeStruct(element_load.shape, f32),
            in_specs=[vmem, vmem],
            out_specs=vmem,
            scratch_shapes=[
                pltpu.VMEM((gx - 1,) + element_load.shape, f32),
                pltpu.VMEM((gx - 1, 8, 128), f32),
                pltpu.VMEM((8, 128), f32),
                pltpu.VMEM((phases, 2, 2, 3, 8, lanes), f32),
                pltpu.VMEM((phases, 2, 2, 3, 8, lanes), f32),
                pltpu.VMEM((phases, 2, 2, 8, lanes), f32),
                pltpu.VMEM((phases, 2, 2, 8, lanes), f32),
                pltpu.VMEM((phases, 4, 8, lanes), f32),
                pltpu.VMEM((phases, 4, 8, lanes), f32),
                pltpu.SemaphoreType.DMA((phases, 8)),
                pltpu.SemaphoreType.DMA((phases, 8)),
                pltpu.SemaphoreType.DMA((2, gx - 1)),
                pltpu.SemaphoreType.DMA((2, gx - 1)),
                pltpu.VMEM((2 * lanes, lanes), jnp.bfloat16),
                pltpu.VMEM((2 * lanes, 256), jnp.bfloat16),
                pltpu.VMEM((wide_z, 3, 32, lanes), f32),
                pltpu.SemaphoreType.DMA((wide_z, 3)),
                pltpu.SemaphoreType.DMA((wide_z, 3)),
                pltpu.VMEM((8, 32, 128), f32),
                pltpu.VMEM((8, gx, 32, 128), f32),
                pltpu.SemaphoreType.DMA((8, gx)),
                pltpu.SemaphoreType.DMA((8, gx)),
                pltpu.VMEM((gx,) + element_load.shape, f32),
            ],
            compiler_params=pltpu.CompilerParams(
                collective_id=0, has_side_effects=True, vmem_limit_bytes=48 * 1024 * 1024
            ),
        )(element_load, conductivity)

    spec = P("gz", "gy", "gx")
    return jax.shard_map(
        step, mesh=mesh, in_specs=(spec, spec), out_specs=spec, check_vma=False
    )
```

```python
import functools

import jax
import jax.numpy as jnp
from jax import lax
from jax.experimental import pallas as pl
from jax.experimental.pallas import tpu as pltpu
from jax.sharding import PartitionSpec as P

DEG1 = 3
DEG2 = 4
REACTION = 0.05
LOWER = 0.25
UPPER = 2.5
EIG = (0.0, 12.0, 60.0)
W = (1.0 / 36.0, 1.0 / 12.0, 1.0 / 45.0)
MESH = pl.DeviceIdType.MESH
STEPS = ((1, 0), (-1, 0), (0, 1), (0, -1), (1, 1), (1, -1), (-1, 1), (-1, -1))


def iota(shape, dim):
    return lax.broadcasted_iota(jnp.int32, shape, dim)


def pieces(v):
    high = v.astype(jnp.bfloat16).astype(jnp.float32)
    rest = v - high
    mid = rest.astype(jnp.bfloat16).astype(jnp.float32)
    return [high, mid, rest - mid]


def dot_right(v, matrix):
    n = v.shape[0]
    tall = jnp.concatenate(pieces(v), 0).astype(jnp.bfloat16)
    out = jnp.dot(tall, matrix, preferred_element_type=jnp.float32)
    return out[2 * n :] + out[n : 2 * n] + out[:n]


def dot_left(matrix, v):
    tall = jnp.concatenate(pieces(v), 0).astype(jnp.bfloat16)
    wide = jnp.concatenate([matrix] * 3, 1).astype(jnp.bfloat16)
    return jnp.dot(wide, tall, preferred_element_type=jnp.float32)


def weight(d, odd):
    a = jnp.abs(d)
    even_w = jnp.where(a == 0, 1.0, jnp.where(a == 1, 0.375, jnp.where(a == 3, -0.125, 0.0)))
    odd_w = jnp.where(a == 0, 1.0, jnp.where(a == 1, 0.75, 0.0))
    return jnp.where(odd, odd_w, even_w)


def wrapped(d, period):
    d = jnp.where(d > period // 2, d - period, d)
    return jnp.where(d < -(period // 2), d + period, d)


def bits(n):
    return n.bit_length() - 1


def split_matrix(lanes):
    n = 2 * lanes
    r, c = iota((n, n), 0), iota((n, n), 1)
    return jnp.where(r == 2 * (c & (lanes - 1)) + (c >> bits(lanes)), 1.0, 0.0).astype(jnp.bfloat16)


def place_matrix(lanes):
    r, c = iota((2 * lanes, 3 * lanes), 0), iota((2 * lanes, 3 * lanes), 1)
    layer, e = (r >> 6) & 1, ((r >> 7) << 6) + (r & 63)
    block, at = c >> bits(lanes), c & (lanes - 1)
    hit = ((block == layer) & (e == at)) | ((block == 2) & ((e >> 1) == (at & (lanes // 2 - 1))))
    return jnp.where(hit, 1.0, 0.0).astype(jnp.bfloat16)


def restrict_matrix(lanes):
    n = 2 * lanes
    r, c = iota((n, lanes), 0), iota((n, lanes), 1)
    node = 2 * (r & (lanes - 1)) + (r >> bits(lanes))
    cp, m = c >> bits(lanes // 2), c & (lanes // 2 - 1)
    return weight(wrapped(node - 4 * m - 2 * cp, n), cp == 1).astype(jnp.bfloat16)


def out_matrix(lanes):
    n = 2 * lanes
    r, c = iota((n, 128), 0), iota((n, 128), 1)
    m, cp = r & (lanes - 1), r >> bits(lanes)
    merge = jnp.where(2 * m + cp == c, 1.0, 0.0)
    prolong = jnp.where(
        m < lanes // 2, weight(wrapped(c - 4 * m - 2 * cp, n), cp == 1), 0.0
    )
    return jnp.concatenate([merge, prolong], 1).astype(jnp.bfloat16)


def fine_row(r):
    kind, i = r >> 3, r & 7
    return jnp.where(kind == 2, jnp.where(i == 7, 16, 1000), 2 * i + kind)


def packet_matrix():
    r, c = iota((32, 24), 0), iota((32, 24), 1)
    kind, i = (r & 7) >> 2, r & 3
    end = r >= 24
    at = jnp.where(end, 16, 4 * i + 2 * kind)
    layer = jnp.where(end, r - 24, r >> 3)
    values = jnp.where(end, weight(fine_row(c) - at, False), weight(fine_row(c) - at, kind == 1))
    blocks = [jnp.where(layer == l, values, 0.0) for l in range(3)]
    r, c = iota((32, 8), 0), iota((32, 8), 1)
    return jnp.concatenate(blocks + [jnp.where((c >> 1) == r - 27, 0.125, 0.0)], 1)


def window_matrix():
    r, c = iota((112, 96), 0), iota((112, 96), 1)
    l, kind, slot, i = r >> 5, (r & 31) >> 4, (r & 15) >> 2, r & 3
    at, k = c >> 5, c & 31
    body = (at == slot) & (k == 8 * l + 4 * kind + i)
    end = (kind == 0) & (i == 0) & (at == slot - 1) & (k == 24 + l)
    cells = (at == slot) & (k == 27 + i)
    return jnp.where(((r < 96) & (body | end)) | ((r >= 96) & cells), 1.0, 0.0)


def out_rows():
    r, c = iota((24, 24), 0), iota((24, 24), 1)
    merge = jnp.where(fine_row(c) == r, 1.0, 0.0)
    r, c = iota((24, 32), 0), iota((24, 32), 1)
    odd = c >= 16
    e = c & 15
    inside = (e >= 4) & (e <= jnp.where(odd, 7, 8))
    at = 4 * (e - 4) + jnp.where(odd, 2, 0)
    prolong = jnp.where(inside, weight(r - at, odd), 0.0)
    return jnp.concatenate([merge, prolong], 1)


def roll_x(v, step):
    lanes = v.shape[-1]
    return pltpu.roll(v.reshape(-1, lanes), step % lanes, 1).reshape(v.shape)


def roll_y(v, step):
    flat = v.reshape((-1,) + v.shape[-2:])
    return pltpu.roll(flat, step % v.shape[-2], 1).reshape(v.shape)


def forward(a, b, c):
    s = a + c
    return s + 4.0 * b, a - c, s - 2.0 * b


def backward(a, b, c, squared):
    s = a + c
    if squared:
        return s + b, 16.0 * a + 4.0 * c, s + b
    return s + b, 4.0 * a - 2.0 * c, s - b


def factors(cond, h):
    cells = cond.shape[0]
    out = []
    for l in range(3):
        rows = []
        for z in range(cells):
            for j in range(3):
                for i in range(3):
                    w = W[i] * W[j] * W[l]
                    rows.append(
                        cond[z] * (w * h * (EIG[i] + EIG[j] + EIG[l])) + w * REACTION * h**3
                    )
        out.append(jnp.stack(rows, 0).reshape((cells, 3, 3) + cond.shape[1:]))
    return out


def to_nodes(modes, squared=False):
    cells = modes[0].shape[0]
    row = iota(modes[0].shape[-2:], 0)
    low, mid, up = backward(*modes, squared)
    layers = [low[0]]
    for z in range(cells):
        layers.append(mid[z])
        layers.append(up[z] + low[z + 1] if z + 1 < cells else up[z])
    q = jnp.stack(layers, 0)
    low, mid, up = backward(q[:, 0], q[:, 1], q[:, 2], squared)
    even = low + jnp.where(row == 0, 0.0, roll_y(up, 1))
    q = jnp.stack([even, mid, up], 2)
    low, mid, up = backward(q[:, 0], q[:, 1], q[:, 2], squared)
    return low + roll_x(up, 1), mid


def apply_local(field, factor, ny):
    even, odd = field
    cells = factor[0].shape[0]
    row = iota(even.shape[-2:], 0)
    g = jnp.stack(forward(even, odd, roll_x(even, -1)), 0)
    low, mid, end = g[:, :, 0], g[:, :, 1], g[:, :, 2]
    up = jnp.where(row == ny - 1, end, roll_y(low, -1))
    y = jnp.stack(forward(low, mid, up), 0)
    parts = [jnp.stack([y[:, :, 2 * z + a] for z in range(cells)], 0) for a in range(3)]
    modes = forward(*parts)
    return to_nodes([m * f for m, f in zip(modes, factor)])


def window_nodes(modes, squared=False):
    cells = modes[0].shape[0]
    low, mid, up = backward(*modes, squared)
    layers = []
    for z in range(cells):
        layers += [low[z] + up[z - 1], mid[z]]
    q = jnp.stack(layers, 0)
    low, mid, up = backward(q[:, 0], q[:, 1], q[:, 2], squared)
    q = jnp.stack([low + roll_y(up, 1), mid], 2)
    low, mid, up = backward(q[:, 0], q[:, 1], q[:, 2], squared)
    return low + roll_x(up, 1), mid


def apply_window(field, factor):
    even, odd = field
    cells = factor[0].shape[0]
    g = jnp.stack(forward(even, odd, roll_x(even, -1)), 0)
    low, mid = g[:, :, 0], g[:, :, 1]
    y = jnp.stack(forward(low, mid, roll_y(low, -1)), 0)
    parts = [
        jnp.stack([y[:, :, (2 * z + a) % (2 * cells)] for z in range(cells)], 0)
        for a in range(3)
    ]
    modes = forward(*parts)
    return window_nodes([m * f for m, f in zip(modes, factor)])


def exchange(fields, phase, ny, bufs, beside=None):
    zs, zr, ys, yr, cs, cr, send_sem, recv_sem = bufs
    flat = [part for field in fields for part in field]
    count = len(flat)
    layers = flat[0].shape[0]
    last = layers - 1
    row = iota(flat[0].shape[-2:], 0)
    for f, part in enumerate(flat):
        for d, l in enumerate((last, 0)):
            zs[phase, d, 2 * f : 2 * f + 2] = part[l, 0:2]
            zs[phase, d, 4, f : f + 1] = part[l, 2, ny - 1 : ny]
        for l in range(layers):
            ys[phase, 0, f, l : l + 1] = part[l, 2, ny - 1 : ny]
            ys[phase, 1, f, l : l + 1] = part[l, 0, 0:1]
        cs[phase, 0, f : f + 1] = part[last, 2, ny - 1 : ny]
        cs[phase, 1, f : f + 1] = part[0, 2, ny - 1 : ny]
        cs[phase, 2, f : f + 1] = part[last, 0, 0:1]
        cs[phase, 3, f : f + 1] = part[0, 0, 0:1]
    gy, gz = lax.axis_size("gy"), lax.axis_size("gz")
    iy, iz = lax.axis_index("gy"), lax.axis_index("gz")
    copies = []
    for k in (2, 3, 0, 1, 4, 5, 6, 7):
        dy, dz = STEPS[k]
        if k < 2:
            src, dst = ys.at[phase, k, pl.ds(0, count)], yr.at[phase, k, pl.ds(0, count)]
        elif k < 4:
            src, dst = zs.at[phase, k - 2], zr.at[phase, k - 2]
        else:
            src, dst = cs.at[phase, k - 4], cr.at[phase, k - 4]
        copy = pltpu.make_async_remote_copy(
            src_ref=src,
            dst_ref=dst,
            send_sem=send_sem.at[phase, k],
            recv_sem=recv_sem.at[phase, k],
            device_id={"gy": lax.rem(iy + dy + gy, gy), "gz": lax.rem(iz + dz + gz, gz)},
            device_id_type=MESH,
        )
        copy.start()
        copies.append(copy)
    if beside is not None:
        beside()
    for copy in copies:
        copy.wait_recv()
    out = []
    for f, part in enumerate(flat):
        done = []
        for l in range(layers):
            first = yr[phase, 0, f, l : l + 1]
            end = yr[phase, 1, f, l : l + 1]
            if l == last:
                first = first + cr[phase, 1, f : f + 1]
                end = end + cr[phase, 3, f : f + 1]
            if l == 0:
                first = first + cr[phase, 0, f : f + 1]
                end = end + cr[phase, 2, f : f + 1]
            low, mid = part[l, 0], part[l, 1]
            if l in (0, last):
                d = 0 if l == 0 else 1
                end = end + zr[phase, d, 4, f : f + 1]
                low, mid = low + zr[phase, d, 2 * f], mid + zr[phase, d, 2 * f + 1]
            low = low + jnp.where(row == 0, first, 0.0)
            done.append(jnp.stack([low, mid, part[l, 2] + end], 0))
        out.append(jnp.stack(done, 0))
    return [(out[2 * i], out[2 * i + 1]) for i in range(len(fields))], copies


def fine_diagonal(cells, below, above):
    row = iota(cells.shape[-2:], 0)
    mass, stiff = (4.0 / 30.0, 16.0 / 30.0), (7.0 / 3.0, 16.0 / 3.0)
    out = []
    for x in range(2):
        v, lo, hi = cells, below, above
        if x == 0:
            v, lo, hi = (t + roll_x(t, 1) for t in (v, lo, hi))
        rows = ((v + jnp.where(row == 0, lo, roll_y(v, 1)), 0), (v, 1), (v + hi, 0))
        parts = []
        for z in range(5):
            for t, y in rows:
                near = t[z // 2 + 1] if z % 2 else t[z // 2] + t[z // 2 + 1]
                k = (x, y, z % 2)
                m = [mass[i] for i in k]
                w = [stiff[i] for i in k]
                share = w[0] * m[1] * m[2] + m[0] * w[1] * m[2] + m[0] * m[1] * w[2]
                count = 2 ** (3 - sum(k))
                parts.append(near * share + REACTION * m[0] * m[1] * m[2] * count)
        out.append(jnp.stack(parts, 0).reshape((5, 3) + cells.shape[1:]))
    return out


def inverse(diagonal, ny):
    row = iota(diagonal.shape[-2:], 0)
    whole = jnp.where(row < ny, 1.0 / diagonal[:, 0:2], 0.0)
    end = jnp.where(row == ny - 1, 1.0 / diagonal[:, 2:3], 0.0)
    return jnp.concatenate([whole, end], 1)


def chebyshev(right, scaled, operate, degree):
    centre = 0.5 * (UPPER + LOWER)
    half = 0.5 * (UPPER - LOWER)
    sharp = centre / half
    f = 1.0 / sharp
    update = [s * r * (1.0 / centre) for s, r in zip(scaled, right)]
    total = update
    for k in range(1, degree):
        image = operate(total, k)
        g = 1.0 / (2.0 * sharp - f)
        update = [
            (g * f) * u + (2.0 * g / half) * (s * (r - a))
            for u, s, r, a in zip(update, scaled, right, image)
        ]
        total = [t + u for t, u in zip(total, update)]
        f = g
    return total


def kernel(load_ref, cond_ref, out_ref, line, cells, cell_out, zs, zr, ys, yr, cs, cr,
           send_sem, recv_sem, x_send, x_recv, matrix_x, matrix_out,
           packets, w_send, w_recv, near, far, n_send, n_recv, summed):
    gx, gy, gz = lax.axis_size("gx"), lax.axis_size("gy"), lax.axis_size("gz")
    ix, iy, iz = lax.axis_index("gx"), lax.axis_index("gy"), lax.axis_index("gz")
    lanes = 64 * gx
    bufs = (zs, zr, ys, yr, cs, cr, send_sem, recv_sem)
    barrier = pltpu.get_barrier_semaphore()
    wide_z = packets.shape[0]
    own_z = wide_z // 2
    slots = [
        (z, y) for z in range(wide_z) for y in range(3) if (z, y) != (own_z, 1)
    ]

    def holder(slot):
        return {
            "gy": lax.rem(iy + 1 - slot[1] + gy, gy),
            "gz": lax.rem(iz + own_z - slot[0] + gz, gz),
        }

    def beside(step, d):
        return {
            "gx": lax.rem(ix + d, gx),
            "gy": lax.rem(iy + step[0] + gy, gy),
            "gz": lax.rem(iz + step[1] + gz, gz),
        }

    for slot in slots:
        pl.semaphore_signal(barrier, inc=1, device_id=holder(slot), device_id_type=MESH)
    for step in STEPS:
        for d in range(1, gx):
            pl.semaphore_signal(barrier, inc=1, device_id=beside(step, d), device_id_type=MESH)
    for d in range(1, gx):
        pl.semaphore_signal(
            barrier, inc=1, device_id={"gx": lax.rem(ix + d, gx)}, device_id_type=MESH
        )
    cell_out[:, 0:64] = cond_ref[0]
    cell_out[:, 64:128] = cond_ref[1]
    for k, (dy, dz) in enumerate(STEPS):
        y, z = (16 if dy == 1 else 0), (4 if dz == 1 else 0)
        if dy == 0:
            near[k, 0:17] = load_ref[z]
            near[k, 24:32] = cell_out[...]
        else:
            for l in range(5) if dz == 0 else (0,):
                near[k, l : l + 1] = load_ref[l if dz == 0 else z, y : y + 1]
            near[k, 5:6] = cell_out[7:8] if dy == 1 else cell_out[0:1]
    pl.semaphore_wait(barrier, len(slots) + 9 * (gx - 1))
    started = []
    arrivals = []
    for d in range(1, gx):
        for k, (src, dst) in enumerate(((load_ref, line), (cell_out, cells))):
            copy = pltpu.make_async_remote_copy(
                src_ref=src,
                dst_ref=dst.at[gx - d - 1],
                send_sem=x_send.at[k, d - 1],
                recv_sem=x_recv.at[k, gx - d - 1],
                device_id={"gx": lax.rem(ix + d, gx)},
                device_id_type=MESH,
            )
            copy.start()
            arrivals.append(copy)
    for k in (4, 5, 6, 7, 2, 3, 0, 1):
        count = 32 if STEPS[k][0] == 0 else 8
        for d in range(gx):
            copy = pltpu.make_async_remote_copy(
                src_ref=near.at[k, pl.ds(0, count)],
                dst_ref=far.at[k, (gx - d) % gx, pl.ds(0, count)],
                send_sem=n_send.at[k, d],
                recv_sem=n_recv.at[k, (gx - d) % gx],
                device_id=beside(STEPS[k], d),
                device_id_type=MESH,
            )
            copy.start()
            arrivals.append(copy)
    matrix_x[...] = restrict_matrix(lanes)
    matrix_out[...] = out_matrix(lanes)
    split_x, place = split_matrix(lanes), place_matrix(lanes)
    for copy in arrivals:
        copy.wait_recv()
    started += arrivals

    def rows(ref):
        parts = []
        for z in range(5):
            parts.append(ref[z, pl.ds(0, 8, stride=2), :])
            parts.append(ref[z, pl.ds(1, 8, stride=2), :])
            parts.append(jnp.broadcast_to(ref[z, 16:17, :], (8, 128)))
        return jnp.concatenate(parts, 0)

    bricks = [load_ref] + [line.at[d] for d in range(gx - 1)]
    for g, brick in enumerate(bricks):
        for z in range(5):
            v = brick[z]
            first, end = far[0, g, z : z + 1], far[1, g, z : z + 1]
            if z == 0:
                v = v + far[2, g, 0:17]
                first, end = first + far[4, g, 0:1], end + far[6, g, 0:1]
            if z == 4:
                v = v + far[3, g, 0:17]
                first, end = first + far[5, g, 0:1], end + far[7, g, 0:1]
            summed[g, z] = v
            summed[g, z, 0:1] = v[0:1] + first
            summed[g, z, 16:17] = v[16:17] + end
    joined = jnp.concatenate(
        [
            jnp.concatenate([rows(b) for b in bricks], 1),
            jnp.concatenate([rows(summed.at[g]) for g in range(gx)], 1),
        ],
        0,
    )
    loads = dot_right(joined, split_x).reshape(2, 5, 3, 8, 2 * lanes)
    load, right = (
        (loads[i, :, :, :, :lanes], loads[i, :, :, :, lanes:]) for i in range(2)
    )
    owned = [cell_out] + [cells.at[d] for d in range(gx - 1)]
    joined = jnp.concatenate(
        [
            jnp.concatenate(
                [owned[g][...], far[2, g, 24:32], far[3, g, 24:32]]
                + [far[k, g, 0:8] for k in (0, 1, 4, 5, 6, 7)],
                0,
            )
            for g in range(gx)
        ],
        1,
    )
    conds = dot_right(joined, place)

    def one(at, layer):
        row = conds[at + 5 : at + 6, layer * lanes : (layer + 1) * lanes]
        return jnp.broadcast_to(row, (8, lanes))

    cond = jnp.stack([conds[0:8, :lanes], conds[0:8, lanes : 2 * lanes]], 0)
    around = jnp.stack(
        [conds[8:16, lanes : 2 * lanes], cond[0], cond[1], conds[16:24, :lanes]], 0
    )
    below = jnp.stack([one(40, 1), one(24, 0), one(24, 1), one(48, 0)], 0)
    above = jnp.stack([one(56, 1), one(32, 0), one(32, 1), one(64, 0)], 0)
    pair = conds[0:8, 2 * lanes :]
    fine = factors(cond, 1.0)
    diagonal = fine_diagonal(around, below, above)

    def operate(field, k):
        (image,), copies = exchange([apply_local(field, fine, 8)], k - 1, 8, bufs)
        started.extend(copies)
        return image

    smooth = chebyshev(right, [inverse(d, 8) for d in diagonal], operate, DEG1)
    image = apply_local(smooth, fine, 8)
    part = [
        jnp.concatenate([(b - a).reshape(5, 24, lanes) for b, a in zip(load, image)], 2)
    ][0]
    f0, f1, f2, f3, f4 = (part[z] for z in range(5))
    three = jnp.concatenate(
        [
            f0 + 0.375 * f1 - 0.125 * f3,
            0.75 * f1 + f2 + 0.75 * f3,
            -0.125 * f1 + 0.375 * f3 + f4,
        ],
        0,
    )
    three = dot_right(three, matrix_x[...])
    packets[own_z, 1] = dot_left(packet_matrix(), jnp.concatenate([three, pair], 0))
    copies = []
    for slot in slots:
        copy = pltpu.make_async_remote_copy(
            src_ref=packets.at[own_z, 1],
            dst_ref=packets.at[slot],
            send_sem=w_send.at[slot],
            recv_sem=w_recv.at[slot],
            device_id=holder(slot),
            device_id_type=MESH,
        )
        copy.start()
        copies.append(copy)
    started += copies
    own = jnp.concatenate([s.reshape(120, lanes) for s in smooth], 1)
    own = dot_right(own, matrix_out[:, :128])
    gather = window_matrix()
    for copy in copies:
        copy.wait_recv()
    tall = [
        jnp.concatenate([packets[z, y] for y in range(3)], 0) for z in range(wide_z)
    ]
    tall = dot_left(gather, jnp.concatenate(tall, 1))
    tall = [tall[:, z * lanes : (z + 1) * lanes] for z in range(wide_z)]
    layers = []
    for z in range(wide_z):
        layers += [tall[z][0:32] + tall[z - 1][64:96], tall[z][32:64]]
    packed = jnp.stack(layers, 0).reshape(2 * wide_z, 2, 16, lanes)
    turned = roll_x(packed, lanes // 2)
    first = iota(packed.shape[-2:], 1) < lanes // 2
    right = (jnp.where(first, packed, turned), jnp.where(first, turned, packed))
    coarse = factors(jnp.stack([t[96:112] for t in tall], 0), 2.0)
    diagonal = window_nodes(coarse, True)
    correction = chebyshev(
        right, [1.0 / d for d in diagonal], lambda v, k: apply_window(v, coarse), DEG2
    )
    c0, c1, c2 = (
        jnp.concatenate([v[(2 * own_z + l) % (2 * wide_z)].reshape(32, lanes) for v in correction], 1)
        for l in range(3)
    )
    five = jnp.concatenate(
        [
            c0,
            0.375 * c0 + 0.75 * c1 - 0.125 * c2,
            c1,
            -0.125 * c0 + 0.75 * c1 + 0.375 * c2,
            c2,
        ],
        0,
    )
    five = dot_right(five, matrix_out[:, 128:])
    tall = jnp.concatenate(
        [
            jnp.concatenate([v[n * z : n * z + n] for z in range(5)], 1)
            for v, n in ((own, 24), (five, 32))
        ],
        0,
    )
    result = dot_left(out_rows(), tall)
    for z in range(5):
        out_ref[z] = result[0:17, 128 * z : 128 * z + 128]
    for copy in started:
        copy.wait_send()


def solution(mesh):
    gx = mesh.shape["gx"]
    lanes = 64 * gx
    phases = DEG1 - 1
    wide_z = min(mesh.shape["gz"], 9)

    def step(element_load, conductivity):
        vmem = pl.BlockSpec(memory_space=pltpu.VMEM)
        f32 = jnp.float32
        return pl.pallas_call(
            kernel,
            out_shape=jax.ShapeDtypeStruct(element_load.shape, f32),
            in_specs=[vmem, vmem],
            out_specs=vmem,
            scratch_shapes=[
                pltpu.VMEM((gx - 1,) + element_load.shape, f32),
                pltpu.VMEM((gx - 1, 8, 128), f32),
                pltpu.VMEM((8, 128), f32),
                pltpu.VMEM((phases, 2, 5, 8, lanes), f32),
                pltpu.VMEM((phases, 2, 5, 8, lanes), f32),
                pltpu.VMEM((phases, 2, 2, 8, lanes), f32),
                pltpu.VMEM((phases, 2, 2, 8, lanes), f32),
                pltpu.VMEM((phases, 4, 8, lanes), f32),
                pltpu.VMEM((phases, 4, 8, lanes), f32),
                pltpu.SemaphoreType.DMA((phases, 8)),
                pltpu.SemaphoreType.DMA((phases, 8)),
                pltpu.SemaphoreType.DMA((2, gx - 1)),
                pltpu.SemaphoreType.DMA((2, gx - 1)),
                pltpu.VMEM((2 * lanes, lanes), jnp.bfloat16),
                pltpu.VMEM((2 * lanes, 256), jnp.bfloat16),
                pltpu.VMEM((wide_z, 3, 32, lanes), f32),
                pltpu.SemaphoreType.DMA((wide_z, 3)),
                pltpu.SemaphoreType.DMA((wide_z, 3)),
                pltpu.VMEM((8, 32, 128), f32),
                pltpu.VMEM((8, gx, 32, 128), f32),
                pltpu.SemaphoreType.DMA((8, gx)),
                pltpu.SemaphoreType.DMA((8, gx)),
                pltpu.VMEM((gx,) + element_load.shape, f32),
            ],
            compiler_params=pltpu.CompilerParams(
                collective_id=0, has_side_effects=True, vmem_limit_bytes=48 * 1024 * 1024
            ),
        )(element_load, conductivity)

    spec = P("gz", "gy", "gx")
    return jax.shard_map(
        step, mesh=mesh, in_specs=(spec, spec), out_specs=spec, check_vma=False
    )
```
